512 devices in a mesh: image: 32 (over z, core), band: 16 (over y, x).
Axes of the slice: x: 4, y: 4, z: 16, core: 2. Of those that a mesh axis runs over, the one named last changes fastest.
Arguments:
- images: float32 [32, 128, 64, 128], P('image', None, 'band'), may hold values from -60 to 60, as said below
- cotangent: float32 [32, 128, 64, 128], P('image', None, 'band'), may hold values from -6 to 6
- filters: float32 [2, 1152, 128], replicated, may hold values from -6 to 6
- rates: float32 [2], replicated, may hold values from 0.002 to 0.008
Outputs:
- new_filters: float32 [32, 2, 1152, 128], P('image')
The draws below stay inside these ranges and needn't reach their ends.
Inputs may be any that keep to these rules, and one draw needn't show every extreme that they name: `images`: Real-valued feature maps whose channels differ in scale.
All inputs are finite; a program needn't handle non-finite values.
Results may differ from the reference program's by a relative error of at most 0.0001.
Values sent between devices are 32-bit elements; how exact they have to be, the bound alone decides.
A program may use at most 64 MiB of HBM per device.

```python
import math
import jax
import jax.numpy as jnp
from jax import lax

C = 128
COLS = 128
IMAGES = 32
HEIGHT = 64
N_IMAGE = 32


def draw_images(key, part):
    key_scale = jax.random.fold_in(key, 11)
    key_value = jax.random.fold_in(key, 23)
    levels = (jnp.arange(C, dtype=jnp.float32) + jax.random.uniform(key_scale, (C,), jnp.float32)) / C
    channel_scale = 10.0 ** levels
    values = jax.random.normal(key_value, (IMAGES, C, HEIGHT, COLS), jnp.float32)
    return jnp.clip(values * channel_scale[None, :, None, None], -60.0, 60.0)


def block_levels(key, extent, cuts, least, high):
    def one(axis_at, parts):
        steps = jax.random.uniform(jax.random.fold_in(jax.random.fold_in(key, 6), axis_at), (parts,), jnp.float32, least / len(cuts), high / len(cuts))
        return jnp.repeat(jnp.exp(steps), extent[axis_at] // parts).reshape((-1,) + (1,) * (len(extent) - axis_at - 1))

    level = one(*cuts[0])
    for cut in cuts[1:]:
        level = level * one(*cut)
    return level


def gaussian(key, extent, spread, bound, cuts=(), held_as=jnp.bfloat16):
    drawn = spread * jax.random.normal(key, extent, jnp.float32)
    if cuts:
        drawn = drawn * block_levels(key, extent, cuts, -0.22, 0.18)
    return jnp.clip(drawn, -bound, bound).astype(held_as)


def setup_inputs(seed: int = 0) -> dict:
    keys = jax.random.split(jax.random.key(seed), 5)
    images = draw_images(jax.random.fold_in(keys[4], 71), 0)
    cotangent = gaussian(keys[1], (IMAGES, C, HEIGHT, COLS), 1.0, 6.0, ((0, 32), (2, 16)), jnp.float32)
    filters = gaussian(keys[2], (2, 9 * C, C), 1.0, 6.0, (), jnp.float32)
    rates = jnp.clip(jnp.exp(jax.random.uniform(keys[3], (2,), jnp.float32, math.log(0.002), math.log(0.008))), 0.002, 0.008)
    return {"images": images, "cotangent": cotangent, "filters": filters, "rates": rates}


HIGH = lax.Precision.HIGHEST


def taps(padded, rows, cols):
    chans = padded.shape[0]
    pieces = [padded[:, dr:dr + rows, dc:dc + cols] for dr in range(3) for dc in range(3)]
    return jnp.stack(pieces, axis=1).reshape(chans * 9, rows * cols)


def flipped(padded, rows, cols):
    chans = padded.shape[0]
    pieces = [padded[:, 2 - dr:2 - dr + rows, 2 - dc:2 - dc + cols] for dr in range(3) for dc in range(3)]
    return jnp.stack(pieces, axis=1).reshape(chans, 9, rows * cols)


def reference(images, cotangent, filters, rates):
    chans = images.shape[1]
    height = images.shape[2]
    cols = images.shape[3]
    scale = (9 * chans) ** -0.5

    def image_grads(pair):
        feats, cot = pair
        first = jnp.pad(feats, ((0, 0), (1, 1), (1, 1)))
        patch_one = taps(first, height, cols)
        pre = scale * jnp.einsum("kc,kp->cp", filters[0], patch_one, precision=HIGH)
        hidden = jax.nn.silu(pre).reshape(chans, height, cols)
        patch_two = taps(jnp.pad(hidden, ((0, 0), (1, 1), (1, 1))), height, cols)
        flat_cot = cot.reshape(chans, height * cols)
        grad_two = scale * jnp.einsum("kp,cp->kc", patch_two, flat_cot, precision=HIGH)
        back = flipped(jnp.pad(cot, ((0, 0), (1, 1), (1, 1))), height, cols)
        weight_two = filters[1].reshape(chans, 9, chans)
        dhidden = scale * jnp.einsum("itc,ctp->ip", weight_two, back, precision=HIGH)
        sig = jax.nn.sigmoid(pre)
        dpre = dhidden * sig * (1.0 + pre * (1.0 - sig))
        grad_one = scale * jnp.einsum("kp,cp->kc", patch_one, dpre, precision=HIGH)
        return jnp.stack([grad_one, grad_two])

    grads = lax.map(image_grads, (images, cotangent))
    count = N_IMAGE
    kdim = grads.shape[2]
    levels = count.bit_length() - 1
    for level in range(levels):
        stride = 2 ** level
        view = grads.reshape(count // (2 * stride), 2, stride, 2, kdim, chans)
        lower = view[:, 0]
        upper = view[:, 1]
        inner = jnp.sum(lower * upper, axis=(-2, -1))
        lower_sq = jnp.sum(lower * lower, axis=(-2, -1))
        upper_sq = jnp.sum(upper * upper, axis=(-2, -1))
        coef_low = (1.0 - inner / (2.0 * (lower_sq + 1e-6)))[..., None, None]
        coef_up = (1.0 - inner / (2.0 * (upper_sq + 1e-6)))[..., None, None]
        merged = coef_low * lower + coef_up * upper
        grads = jnp.stack([merged, merged], axis=1).reshape(count, 2, kdim, chans)
    return filters[None] - rates[None, :, None, None] * grads
```

```python
import functools

import jax
import jax.numpy as jnp
from jax import lax
from jax.experimental import pallas as pl
from jax.experimental.pallas import tpu as pltpu
from jax.sharding import PartitionSpec as P

MESH = pl.DeviceIdType.MESH
F32 = jnp.float32
BF16 = jnp.bfloat16
HIGH = lax.Precision.HIGHEST


def remote(src, dst, send, recv, image, band):
    return pltpu.make_async_remote_copy(
        src_ref=src,
        dst_ref=dst,
        send_sem=send,
        recv_sem=recv,
        device_id={"image": image, "band": band},
        device_id_type=MESH,
    )


def halves(v):
    hi = v.astype(BF16)
    return hi, (v - hi.astype(F32)).astype(BF16)


def before(v):
    lane = lax.broadcasted_iota(jnp.int32, v.shape, 1)
    return jnp.where(lane == 0, 0.0, pltpu.roll(v, 1, 1))


def after(v):
    lane = lax.broadcasted_iota(jnp.int32, v.shape, 1)
    return jnp.where(lane == 127, 0.0, pltpu.roll(v, 127, 1))


def nn(a, b):
    return lax.dot_general(a, b, (((1,), (0,)), ((), ())), preferred_element_type=F32)


def nt(a, b):
    return lax.dot_general(a, b, (((1,), (1,)), ((), ())), preferred_element_type=F32)


def partner_sum(h, level):
    bit = 1 << level
    row = lax.broadcasted_iota(jnp.int32, h.shape, 0)
    if bit >= 8:
        blocks = [h[8 * k : 8 * k + 8] for k in range(4)]
        other = jnp.concatenate([blocks[k ^ (bit // 8)] for k in range(4)], axis=0)
    else:
        blocks = []
        for k in range(4):
            v = h[8 * k : 8 * k + 8]
            r = lax.broadcasted_iota(jnp.int32, v.shape, 0)
            blocks.append(jnp.where((r & bit) == 0, pltpu.roll(v, 8 - bit, 0), pltpu.roll(v, bit, 0)))
        other = jnp.concatenate(blocks, axis=0)
    h = h + other
    lane = lax.broadcasted_iota(jnp.int32, h.shape, 1)
    other = jnp.where((lane & bit) == 0, pltpu.roll(h, 128 - bit, 1), pltpu.roll(h, bit, 1))
    return h + other


def adasum_weights(gram):
    row = lax.broadcasted_iota(jnp.int32, gram.shape, 0)
    lane = lax.broadcasted_iota(jnp.int32, gram.shape, 1)
    alpha = jnp.ones((32, 1), F32)
    for level in range(5):
        own = row == lane
        pair = row == (lane ^ (1 << level))
        sq = jnp.where(own, gram, 0.0)
        inner = jnp.where(pair, gram, 0.0)
        u_col = 1.0 - jnp.sum(inner, axis=1, keepdims=True) / (
            2.0 * (jnp.sum(sq, axis=1, keepdims=True) + 1e-6)
        )
        alpha = alpha * u_col
        if level < 4:
            u_row = 1.0 - jnp.sum(inner, axis=0, keepdims=True) / (
                2.0 * (jnp.sum(sq, axis=0, keepdims=True) + 1e-6)
            )
            gram = partner_sum(gram * u_col * u_row, level)
    return alpha


def kernel(
    img, cot, fil, rates, out,
    xbuf, ybuf, xh, xl, yh, yl, w1h, w1l, w2h, w2l, z, dsig, hh, hl,
    ga, gb, oppa, oppb, rawa, rawb, suma, sumb, stage_a, stage_b, lata, latb, sown,
    tiles, gram_z, gram_b, merged, block,
    halo_s, halo_r, rs_s, rs_r, lat_s, lat_r, own_sem,
    c_s, c_r, d1_s, d1_r, d2_s, d2_r, e1_s, e1_r, e2_s, e2_r, f_s, f_r, loc_sem,
):
    m = lax.axis_index("image")
    band = lax.axis_index("band")
    depth, core = m // 2, m % 2
    y, x = band // 4, band % 4
    scale = 1152.0 ** -0.5

    barrier = pltpu.get_barrier_semaphore()

    @pl.loop(1, 16)
    def _(j):
        pl.semaphore_signal(
            barrier, inc=1, device_id={"image": m, "band": (band + j) % 16}, device_id_type=MESH
        )

    @pl.loop(1, 32)
    def _(j):
        pl.semaphore_signal(
            barrier, inc=1, device_id={"image": (m + j) % 32, "band": band}, device_id_type=MESH
        )

    for r in range(4):
        xbuf[:, 128 * (r + 1) : 128 * (r + 2)] = img[pl.ds(r, 128, stride=4), :]
        ybuf[:, 128 * (r + 1) : 128 * (r + 2)] = cot[pl.ds(r, 128, stride=4), :]
    pl.semaphore_wait(barrier, 46)

    def halo(buf, k, up):
        if up:
            return remote(
                buf.at[:, pl.ds(128, 128)], buf.at[:, pl.ds(640, 128)],
                halo_s.at[k], halo_r.at[k], m, band - 1,
            )
        return remote(
            buf.at[:, pl.ds(512, 128)], buf.at[:, pl.ds(0, 128)],
            halo_s.at[k], halo_r.at[k], m, band + 1,
        )

    @pl.when(band > 0)
    def _():
        halo(xbuf, 0, True).start()
        halo(ybuf, 2, True).start()

    @pl.when(band < 15)
    def _():
        halo(xbuf, 1, False).start()
        halo(ybuf, 3, False).start()

    for a in range(3):
        for b in range(3):
            w = fil[0, pl.ds(3 * a + b, 128, stride=9), :]
            hi, lo = halves(w.T)
            w1h[128 * b : 128 * b + 128, 128 * a : 128 * a + 128] = hi
            w1l[128 * b : 128 * b + 128, 128 * a : 128 * a + 128] = lo
            hi, lo = halves(fil[1, pl.ds(3 * a + b, 128, stride=9), :])
            w2h[128 * b : 128 * b + 128, 128 * a : 128 * a + 128] = hi
            w2l[128 * b : 128 * b + 128, 128 * a : 128 * a + 128] = lo

    @pl.when(band == 0)
    def _():
        xbuf[:, 0:128] = jnp.zeros((128, 128), F32)
        ybuf[:, 0:128] = jnp.zeros((128, 128), F32)

    @pl.when(band == 15)
    def _():
        xbuf[:, 640:768] = jnp.zeros((128, 128), F32)
        ybuf[:, 640:768] = jnp.zeros((128, 128), F32)

    @pl.when(band < 15)
    def _():
        halo(xbuf, 0, True).wait_recv()
        halo(ybuf, 2, True).wait_recv()

    @pl.when(band > 0)
    def _():
        halo(xbuf, 1, False).wait_recv()
        halo(ybuf, 3, False).wait_recv()

    for r in range(6):
        cols = slice(128 * r, 128 * r + 128)
        xh[:, cols], xl[:, cols] = halves(xbuf[:, cols])
        yh[:, cols], yl[:, cols] = halves(ybuf[:, cols])

    def stacked(ref, start, width, order):
        return jnp.concatenate([ref[:, 128 * a + start : 128 * a + start + width] for a in order], axis=0)

    def product(wh, wl, vh, vl, order):
        for half in range(2):
            hi = stacked(vh, 256 * half, 256, order)
            lo = stacked(vl, 256 * half, 256, order)
            z[:, 256 * half : 256 * half + 256] = nn(wh[...], hi) + (nn(wh[...], lo) + nn(wl[...], hi))

    product(w1h, w1l, xh, xl, (0, 1, 2))
    for r in range(4):
        cols = slice(128 * r, 128 * r + 128)
        pre = scale * (before(z[0:128, cols]) + z[128:256, cols] + after(z[256:384, cols]))
        sig = 1.0 / (1.0 + jnp.exp(-pre))
        hidden = scale * (pre * sig)
        dsig[:, cols] = (scale * scale) * (sig * (1.0 + pre * (1.0 - sig)))
        for b, v in enumerate((before(hidden), hidden, after(hidden))):
            hh[128 * b : 128 * b + 128, cols], hl[128 * b : 128 * b + 128, cols] = halves(v)

    for b in range(3):
        rows = slice(128 * b, 128 * b + 128)
        hi = stacked(yh, 0, 512, (2, 1, 0))
        lo = stacked(yl, 0, 512, (2, 1, 0))
        part = nt(hh[rows], hi) + (nt(hh[rows], lo) + nt(hl[rows], hi))
        ga[b] = part.reshape(4, 4, 8, 384)

    def ring_ids(axis, step):
        if axis == 0:
            return m, y * 4 + (x + step) % 4
        return m, ((y + step) % 4) * 4 + x

    def part_of(ref, axis, where, half):
        if axis == 0:
            return ref.at[:, pl.ds(2 * half, 2), where]
        return ref.at[:, where, pl.ds(2 * half, 2)]

    def ring_copies(g, opp, raw, summed, axis, base):
        at = x if axis == 0 else y
        right, left = ring_ids(axis, 1), ring_ids(axis, 3)
        far = (at + 2) % 4
        first = [
            remote(part_of(g, axis, far, 0), opp.at[0], rs_s.at[base], rs_r.at[base], *right),
            remote(part_of(g, axis, far, 1), opp.at[1], rs_s.at[base + 1], rs_r.at[base + 1], *left),
            remote(part_of(g, axis, (at + 1) % 4, 1), raw.at[1], rs_s.at[base + 2], rs_r.at[base + 2], *right),
            remote(part_of(g, axis, (at + 3) % 4, 0), raw.at[0], rs_s.at[base + 3], rs_r.at[base + 3], *left),
        ]
        second = [
            remote(opp.at[0], summed.at[0], rs_s.at[base + 4], rs_r.at[base + 4], *right),
            remote(opp.at[1], summed.at[1], rs_s.at[base + 5], rs_r.at[base + 5], *left),
        ]
        return first, second

    def ring_start(first):
        for c in first:
            c.start()

    def ring_pass(g, opp, first, second, axis):
        at = x if axis == 0 else y
        first[0].wait_recv()
        opp[0] += part_of(g, axis, (at + 1) % 4, 0)[...]
        second[0].start()
        first[1].wait_recv()
        opp[1] += part_of(g, axis, (at + 3) % 4, 1)[...]
        second[1].start()

    def ring_finish(g, raw, summed, stage, first, second, axis):
        at = x if axis == 0 else y
        first[2].wait_recv()
        first[3].wait_recv()
        second[0].wait_recv()
        second[1].wait_recv()
        for half in range(2):
            stage[:, pl.ds(2 * half, 2)] = part_of(g, axis, at, half)[...] + (raw[half] + summed[half])

    def last_copies(stage, landing, axis, base):
        at = x if axis == 0 else y
        return [
            remote(
                stage.at[:, (at + step) % 4], landing.at[step - 1],
                lat_s.at[base + step - 1], lat_r.at[base + step - 1], *ring_ids(axis, step),
            )
            for step in (1, 2, 3)
        ]

    ring_a = ring_copies(ga, oppa, rawa, suma, 0, 0)
    ring_start(ring_a[0])

    product(w2h, w2l, yh, yl, (2, 1, 0))
    for r in range(4):
        cols = slice(128 * r, 128 * r + 128)
        dhid = after(z[0:128, cols]) + z[128:256, cols] + before(z[256:384, cols])
        dpre = dhid * dsig[:, cols]
        for b, v in enumerate((after(dpre), dpre, before(dpre))):
            hh[128 * b : 128 * b + 128, cols], hl[128 * b : 128 * b + 128, cols] = halves(v)
    for a in range(3):
        hi, lo = xh[:, 128 * a : 128 * a + 512], xl[:, 128 * a : 128 * a + 512]
        part = nt(hi, hh[...]) + (nt(hi, hl[...]) + nt(lo, hh[...]))
        gb[a] = part.reshape(4, 4, 8, 384)

    ring_b = ring_copies(gb, oppb, rawb, sumb, 1, 6)
    ring_start(ring_b[0])
    ring_pass(ga, oppa, *ring_a, 0)
    ring_pass(gb, oppb, *ring_b, 1)
    ring_finish(ga, rawa, suma, stage_a, *ring_a, 0)
    last_a = last_copies(stage_a, lata, 1, 0)
    ring_start(last_a)
    ring_finish(gb, rawb, sumb, stage_b, *ring_b, 1)
    last_b = last_copies(stage_b, latb, 0, 3)
    ring_start(last_b)
    for c in last_a:
        c.wait_recv()
    sown[1] = stage_a[:, y] + (lata[0] + (lata[1] + lata[2]))
    for c in last_b:
        c.wait_recv()
    sown[0] = stage_b[:, x] + (latb[0] + (latb[1] + latb[2]))

    def tile_copy(layer, k):
        o, lane = k // 3, k % 3
        target = 2 * (k + 7 * layer) + layer
        return target, remote(
            sown.at[layer, o, :, pl.ds(128 * lane, 128)], tiles.at[m],
            c_s.at[9 * layer + k], c_r.at[0], target, band,
        )

    for layer in range(2):
        for k in range(9):
            target, copy = tile_copy(layer, k)

            @pl.when(target != m)
            def _():
                copy.start()

            @pl.when(target == m)
            def _():
                tiles[m] = sown[layer, k // 3, :, 128 * (k % 3) : 128 * (k % 3) + 128]

    mine = depth - 7 * core
    owner = (mine >= 0) & (mine < 9)
    first_owner = 7 * core

    @pl.when(owner)
    def _():
        pltpu.make_async_copy(tiles.at[pl.ds(0, 31)], tiles.at[pl.ds(0, 31)], c_r.at[0]).wait()
        flat = tiles.reshape(256, 128)
        total = jnp.zeros((32, 32), F32)
        for s in range(8):
            v = flat[pl.ds(s, 32, stride=8), :]
            total = total + lax.dot_general(
                v, v, (((1,), (1,)), ((), ())), preferred_element_type=F32, precision=HIGH
            )
        wide = jnp.concatenate([total[8 * q : 8 * q + 8] for q in range(4)], axis=1)
        gram_z[mine] = wide
        for step in range(1, 9):
            to = (mine + step) % 9
            remote(
                gram_z.at[mine], gram_z.at[mine], d1_s.at[step - 1], d1_r.at[0],
                2 * (first_owner + to) + core, band,
            ).start()
        pltpu.make_async_copy(gram_z.at[pl.ds(0, 8)], gram_z.at[pl.ds(0, 8)], d1_r.at[0]).wait()
        gram_b[band] = jnp.sum(gram_z[...], axis=0)

        @pl.loop(1, 16)
        def _(j):
            remote(
                gram_b.at[band], gram_b.at[band], d2_s.at[j - 1], d2_r.at[0], m, (band + j) % 16
            ).start()

        pltpu.make_async_copy(gram_b.at[pl.ds(0, 15)], gram_b.at[pl.ds(0, 15)], d2_r.at[0]).wait()
        packed = jnp.sum(gram_b[...], axis=0)
        rows = [packed if q == 0 else pltpu.roll(packed, 128 - 32 * q, 1) for q in range(4)]
        gram = jnp.concatenate(rows, axis=0)
        lane = lax.broadcasted_iota(jnp.int32, gram.shape, 1)
        alpha = adasum_weights(jnp.where(lane < 32, gram, 0.0))
        lines = [
            jnp.sum(flat[pl.ds(s, 32, stride=8), :] * alpha, axis=0, keepdims=True) for s in range(8)
        ]
        merged[mine] = jnp.concatenate(lines, axis=0)

        @pl.loop(1, 16)
        def _(j):
            remote(
                merged.at[mine], merged.at[mine], e1_s.at[j - 1], e1_r.at[0],
                2 * ((depth + j) % 16) + core, band,
            ).start()

        pltpu.make_async_copy(merged.at[pl.ds(0, 8)], merged.at[pl.ds(0, 8)], e1_r.at[0]).wait()

    @pl.when(jnp.logical_not(owner))
    def _():
        pltpu.make_async_copy(merged.at[pl.ds(0, 9)], merged.at[pl.ds(0, 9)], e1_r.at[0]).wait()

    def to_rows(layer):
        for k in range(9):
            t = k if layer == 0 else 3 * (k % 3) + k // 3
            block[pl.ds(t, 8, stride=9), :] = merged[k]
        start = pl.multiple_of(72 * band, 8)
        block[...] = fil[layer, pl.ds(start, 72), :] - rates[layer] * block[...]

    def spread(layer):
        start = pl.multiple_of(72 * band, 8)
        place = out.at[layer, pl.ds(start, 72)]
        sibling = 2 * depth + 1 - layer
        own = pltpu.make_async_copy(block, place, loc_sem.at[0])
        own.start()

        @pl.loop(1, 16)
        def _(j):
            remote(block, place, e2_s.at[j - 1], e2_r.at[j - 1], m, (band + j) % 16).start()

        pair = remote(block, place, f_s.at[0], f_r.at[0], sibling, band)
        pair.start()
        own.wait()

        @pl.loop(1, 16)
        def _(j):
            source = (band + 16 - j) % 16
            there = out.at[layer, pl.ds(pl.multiple_of(72 * source, 8), 72)]
            remote(block, there, e2_s.at[j - 1], e2_r.at[j - 1], m, band).wait_recv()
            remote(there, there, f_s.at[j], f_r.at[j], sibling, band).start()

        @pl.loop(0, 16)
        def _(j):
            source = (band + 16 - j) % 16
            there = out.at[1 - layer, pl.ds(pl.multiple_of(72 * source, 8), 72)]
            copy = remote(block, there, f_s.at[j], f_r.at[j], sibling, band)
            copy.wait_recv()
            copy.wait_send()

        @pl.loop(1, 16)
        def _(j):
            remote(block, place, e2_s.at[j - 1], e2_r.at[j - 1], m, band).wait_send()

    @pl.when(core == 0)
    def _():
        to_rows(0)
        spread(0)

    @pl.when(core == 1)
    def _():
        to_rows(1)
        spread(1)

    @pl.when(band > 0)
    def _():
        halo(xbuf, 0, True).wait_send()
        halo(ybuf, 2, True).wait_send()

    @pl.when(band < 15)
    def _():
        halo(xbuf, 1, False).wait_send()
        halo(ybuf, 3, False).wait_send()

    for c in (*ring_a[0], *ring_a[1], *ring_b[0], *ring_b[1], *last_a, *last_b):
        c.wait_send()
    for layer in range(2):
        for k in range(9):
            target, copy = tile_copy(layer, k)

            @pl.when(target != m)
            def _():
                copy.wait_send()

    @pl.when(owner)
    def _():
        for step in range(1, 9):
            remote(
                gram_z.at[mine], gram_z.at[mine], d1_s.at[step - 1], d1_r.at[0],
                2 * (first_owner + (mine + step) % 9) + core, band,
            ).wait_send()

        @pl.loop(1, 16)
        def _(j):
            remote(
                gram_b.at[band], gram_b.at[band], d2_s.at[j - 1], d2_r.at[0], m, (band + j) % 16
            ).wait_send()
            remote(
                merged.at[mine], merged.at[mine], e1_s.at[j - 1], e1_r.at[0],
                2 * ((depth + j) % 16) + core, band,
            ).wait_send()


def local(images, cotangent, filters, rates):
    vmem = pl.BlockSpec(memory_space=pltpu.VMEM)
    dma = pltpu.SemaphoreType.DMA
    new = pl.pallas_call(
        kernel,
        out_shape=jax.ShapeDtypeStruct((2, 1152, 128), F32),
        in_specs=[vmem, vmem, vmem, pl.BlockSpec(memory_space=pltpu.SMEM)],
        out_specs=pl.BlockSpec(memory_space=pl.ANY),
        scratch_shapes=[
            pltpu.VMEM((128, 768), F32),
            pltpu.VMEM((128, 768), F32),
            pltpu.VMEM((128, 768), BF16),
            pltpu.VMEM((128, 768), BF16),
            pltpu.VMEM((128, 768), BF16),
            pltpu.VMEM((128, 768), BF16),
            pltpu.VMEM((384, 384), BF16),
            pltpu.VMEM((384, 384), BF16),
            pltpu.VMEM((384, 384), BF16),
            pltpu.VMEM((384, 384), BF16),
            pltpu.VMEM((384, 512), F32),
            pltpu.VMEM((128, 512), F32),
            pltpu.VMEM((384, 512), BF16),
            pltpu.VMEM((384, 512), BF16),
            pltpu.VMEM((3, 4, 4, 8, 384), F32),
            pltpu.VMEM((3, 4, 4, 8, 384), F32),
            *[pltpu.VMEM((2, 3, 2, 8, 384), F32)] * 6,
            *[pltpu.VMEM((3, 4, 8, 384), F32)] * 2,
            *[pltpu.VMEM((3, 3, 8, 384), F32)] * 2,
            pltpu.VMEM((2, 3, 8, 384), F32),
            pltpu.VMEM((32, 8, 128), F32),
            pltpu.VMEM((9, 8, 128), F32),
            pltpu.VMEM((16, 8, 128), F32),
            pltpu.VMEM((9, 8, 128), F32),
            pltpu.VMEM((72, 128), F32),
            dma((4,)), dma((4,)), dma((12,)), dma((12,)), dma((6,)), dma((6,)), dma((1,)),
            dma((18,)), dma((1,)), dma((8,)), dma((1,)), dma((15,)), dma((1,)),
            dma((15,)), dma((1,)), dma((15,)), dma((15,)), dma((16,)), dma((16,)), dma((1,)),
        ],
        compiler_params=pltpu.CompilerParams(
            collective_id=0, has_side_effects=True, vmem_limit_bytes=48 * 1024 * 1024
        ),
        name="adasum_step",
    )(images.reshape(512, 128), cotangent.reshape(512, 128), filters, rates)
    return new[None]


def solution(mesh):
    return jax.shard_map(
        local,
        mesh=mesh,
        in_specs=(P("image", None, "band", None), P("image", None, "band", None), P(), P()),
        out_specs=P("image", None, None, None),
        check_vma=False,
    )
```

```python
import functools

import jax
import jax.numpy as jnp
from jax import lax
from jax.experimental import pallas as pl
from jax.experimental.pallas import tpu as pltpu
from jax.sharding import PartitionSpec as P

MESH = pl.DeviceIdType.MESH
F32 = jnp.float32
BF16 = jnp.bfloat16
HIGH = lax.Precision.HIGHEST


def remote(src, dst, send, recv, image, band):
    return pltpu.make_async_remote_copy(
        src_ref=src,
        dst_ref=dst,
        send_sem=send,
        recv_sem=recv,
        device_id={"image": image, "band": band},
        device_id_type=MESH,
    )


def halves(v):
    hi = v.astype(BF16)
    return hi, (v - hi.astype(F32)).astype(BF16)


def before(v):
    lane = lax.broadcasted_iota(jnp.int32, v.shape, 1)
    return jnp.where(lane == 0, 0.0, pltpu.roll(v, 1, 1))


def after(v):
    lane = lax.broadcasted_iota(jnp.int32, v.shape, 1)
    return jnp.where(lane == 127, 0.0, pltpu.roll(v, 127, 1))


def nn(a, b):
    return lax.dot_general(a, b, (((1,), (0,)), ((), ())), preferred_element_type=F32)


def nt(a, b):
    return lax.dot_general(a, b, (((1,), (1,)), ((), ())), preferred_element_type=F32)


def partner_sum(h, level):
    bit = 1 << level
    if bit >= 8:
        blocks = [h[8 * k : 8 * k + 8] for k in range(4)]
        other = jnp.concatenate([blocks[k ^ (bit // 8)] for k in range(4)], axis=0)
    else:
        blocks = []
        for k in range(4):
            v = h[8 * k : 8 * k + 8]
            r = lax.broadcasted_iota(jnp.int32, v.shape, 0)
            blocks.append(jnp.where((r & bit) == 0, pltpu.roll(v, 8 - bit, 0), pltpu.roll(v, bit, 0)))
        other = jnp.concatenate(blocks, axis=0)
    h = h + other
    lane = lax.broadcasted_iota(jnp.int32, h.shape, 1)
    other = jnp.where((lane & bit) == 0, pltpu.roll(h, 128 - bit, 1), pltpu.roll(h, bit, 1))
    return h + other


def adasum_weights(gram):
    row = lax.broadcasted_iota(jnp.int32, gram.shape, 0)
    lane = lax.broadcasted_iota(jnp.int32, gram.shape, 1)
    alpha = jnp.ones((32, 1), F32)
    for level in range(5):
        own = row == lane
        pair = row == (lane ^ (1 << level))
        sq = jnp.where(own, gram, 0.0)
        inner = jnp.where(pair, gram, 0.0)
        u_col = 1.0 - jnp.sum(inner, axis=1, keepdims=True) / (
            2.0 * (jnp.sum(sq, axis=1, keepdims=True) + 1e-6)
        )
        alpha = alpha * u_col
        if level < 4:
            u_row = 1.0 - jnp.sum(inner, axis=0, keepdims=True) / (
                2.0 * (jnp.sum(sq, axis=0, keepdims=True) + 1e-6)
            )
            gram = partner_sum(gram * u_col * u_row, level)
    return alpha


def thirds(v):
    hi = v.astype(BF16)
    v = v - hi.astype(F32)
    mid = v.astype(BF16)
    return hi, mid, (v - mid.astype(F32)).astype(BF16)


FAR_FIRST = (8, 7, 9, 6, 10, 5, 11, 4, 12, 3, 13, 2, 14, 1, 15)


def kernel(
    img_in, cot_in, fil_in, rates, out,
    img, cot, fil, xedge, yedge, xhalo, yhalo, xh, xl, yh, yl, w1h, w1l, w2h, w2l, z, hh, hl,
    ga, gb, oppa, oppb, rawa, rawb, suma, sumb, stage_a, stage_b, lata, latb, sown,
    held, gram_b, block,
    in_sem, halo_s, halo_r, rs_s, rs_r, lat_s, lat_r,
    c_s, c_r, d_s, d_r, e1_s, e1_r, e2_s, e2_r, f_s, f_r, loc_sem,
):
    m = lax.axis_index("image")
    band = lax.axis_index("band")
    depth, core = m // 2, m % 2
    y, x = band // 4, band % 4
    scale = 1152.0 ** -0.5

    barrier = pltpu.get_barrier_semaphore()

    @pl.loop(1, 16)
    def _(j):
        pl.semaphore_signal(
            barrier, inc=1, device_id={"image": m, "band": (band + j) % 16}, device_id_type=MESH
        )

    @pl.loop(1, 32)
    def _(j):
        pl.semaphore_signal(
            barrier, inc=1, device_id={"image": (m + j) % 32, "band": band}, device_id_type=MESH
        )

    loads = [
        pltpu.make_async_copy(src, dst, in_sem.at[k])
        for k, (src, dst) in enumerate(((img_in, img), (cot_in, cot), (fil_in, fil)))
    ]
    for c in loads:
        c.start()

    for c, field, edge, vh, vl in ((loads[0], img, xedge, xh, xl), (loads[1], cot, yedge, yh, yl)):
        c.wait()
        for r in range(4):
            v = field[pl.ds(r, 128, stride=4), :]
            if r % 3 == 0:
                edge[r // 3] = v
            cols = slice(128 * (r + 1), 128 * (r + 2))
            vh[:, cols], vl[:, cols] = halves(v)

    def halo(edge, landing, k, up):
        if up:
            return remote(edge.at[0], landing.at[1], halo_s.at[k], halo_r.at[k], m, band - 1)
        return remote(edge.at[1], landing.at[0], halo_s.at[k], halo_r.at[k], m, band + 1)

    loads[2].wait()
    for a in range(3):
        for b in range(3):
            rows, cols = slice(128 * b, 128 * b + 128), slice(128 * a, 128 * a + 128)
            w = fil[0, pl.ds(3 * a + b, 128, stride=9), :]
            w1h[rows, cols], w1l[rows, cols] = halves(w.T)
            w2h[rows, cols], w2l[rows, cols] = halves(fil[1, pl.ds(3 * a + b, 128, stride=9), :])

    def columns(ref, pair, offset):
        first, second = (128 * (r + offset) for r in pair)
        return jnp.concatenate([ref[:, first : first + 128], ref[:, second : second + 128]], axis=1)

    def stacked(ref, pair, order):
        return jnp.concatenate([columns(ref, pair, a) for a in order], axis=0)

    def product(wh, wl, hi, lo):
        z[...] = nn(wh[...], hi) + (nn(wh[...], lo) + nn(wl[...], hi))

    def hidden_of(pair):
        product(w1h, w1l, stacked(xh, pair, (0, 1, 2)), stacked(xl, pair, (0, 1, 2)))
        slopes = []
        for q in range(2):
            cols = slice(128 * q, 128 * q + 128)
            pre = scale * (before(z[0:128, cols]) + z[128:256, cols] + after(z[256:384, cols]))
            sig = 1.0 / (1.0 + jnp.exp(-pre))
            hidden = scale * (pre * sig)
            slopes.append((scale * scale) * (sig * (1.0 + pre * (1.0 - sig))))
            for b, v in enumerate((before(hidden), hidden, after(hidden))):
                hh[128 * b : 128 * b + 128, cols], hl[128 * b : 128 * b + 128, cols] = halves(v)
        return slopes

    def second_gradient(pair, add):
        hi, lo = stacked(yh, pair, (2, 1, 0)), stacked(yl, pair, (2, 1, 0))
        for b in range(3):
            rows = slice(128 * b, 128 * b + 128)
            part = nt(hh[rows], hi) + (nt(hh[rows], lo) + nt(hl[rows], hi))
            part = part.reshape(4, 4, 8, 384)
            ga[b] = ga[b] + part if add else part

    def first_gradient(pair, slopes, add):
        product(w2h, w2l, stacked(yh, pair, (2, 1, 0)), stacked(yl, pair, (2, 1, 0)))
        for q in range(2):
            cols = slice(128 * q, 128 * q + 128)
            dpre = (after(z[0:128, cols]) + z[128:256, cols] + before(z[256:384, cols])) * slopes[q]
            for b, v in enumerate((after(dpre), dpre, before(dpre))):
                hh[128 * b : 128 * b + 128, cols], hl[128 * b : 128 * b + 128, cols] = halves(v)
        for a in range(3):
            hi, lo = columns(xh, pair, a), columns(xl, pair, a)
            part = nt(hi, hh[...]) + (nt(hi, hl[...]) + nt(lo, hh[...]))
            part = part.reshape(4, 4, 8, 384)
            gb[a] = gb[a] + part if add else part

    slopes = hidden_of((1, 2))
    second_gradient((1, 2), False)
    first_gradient((1, 2), slopes, False)

    pl.semaphore_wait(barrier, 46)

    @pl.when(band > 0)
    def _():
        halo(xedge, xhalo, 0, True).start()
        halo(yedge, yhalo, 2, True).start()

    @pl.when(band < 15)
    def _():
        halo(xedge, xhalo, 1, False).start()
        halo(yedge, yhalo, 3, False).start()

    @pl.when(band == 0)
    def _():
        xhalo[0] = jnp.zeros((128, 128), F32)
        yhalo[0] = jnp.zeros((128, 128), F32)

    @pl.when(band == 15)
    def _():
        xhalo[1] = jnp.zeros((128, 128), F32)
        yhalo[1] = jnp.zeros((128, 128), F32)

    def halo_arrived(edge, landing, k):
        @pl.when(band < 15)
        def _():
            halo(edge, landing, k, True).wait_recv()

        @pl.when(band > 0)
        def _():
            halo(edge, landing, k + 1, False).wait_recv()

    halo_arrived(xedge, xhalo, 0)
    xh[:, 0:128], xl[:, 0:128] = halves(xhalo[0])
    xh[:, 640:768], xl[:, 640:768] = halves(xhalo[1])
    slopes = hidden_of((0, 3))
    halo_arrived(yedge, yhalo, 2)
    yh[:, 0:128], yl[:, 0:128] = halves(yhalo[0])
    yh[:, 640:768], yl[:, 640:768] = halves(yhalo[1])
    second_gradient((0, 3), True)

    def ring_ids(axis, step):
        if axis == 0:
            return m, y * 4 + (x + step) % 4
        return m, ((y + step) % 4) * 4 + x

    def part_of(ref, axis, where, half):
        if axis == 0:
            return ref.at[:, pl.ds(2 * half, 2), where]
        return ref.at[:, where, pl.ds(2 * half, 2)]

    def ring_copies(g, opp, raw, summed, axis, base):
        at = x if axis == 0 else y
        right, left = ring_ids(axis, 1), ring_ids(axis, 3)
        far = (at + 2) % 4
        first = [
            remote(part_of(g, axis, far, 0), opp.at[0], rs_s.at[base], rs_r.at[base], *right),
            remote(part_of(g, axis, far, 1), opp.at[1], rs_s.at[base + 1], rs_r.at[base + 1], *left),
            remote(part_of(g, axis, (at + 1) % 4, 1), raw.at[1], rs_s.at[base + 2], rs_r.at[base + 2], *right),
            remote(part_of(g, axis, (at + 3) % 4, 0), raw.at[0], rs_s.at[base + 3], rs_r.at[base + 3], *left),
        ]
        second = [
            remote(opp.at[0], summed.at[0], rs_s.at[base + 4], rs_r.at[base + 4], *right),
            remote(opp.at[1], summed.at[1], rs_s.at[base + 5], rs_r.at[base + 5], *left),
        ]
        return first, second

    def ring_start(first):
        for c in first:
            c.start()

    def ring_pass(g, opp, first, second, axis):
        at = x if axis == 0 else y
        first[0].wait_recv()
        opp[0] += part_of(g, axis, (at + 1) % 4, 0)[...]
        second[0].start()
        first[1].wait_recv()
        opp[1] += part_of(g, axis, (at + 3) % 4, 1)[...]
        second[1].start()

    def ring_finish(g, raw, summed, stage, first, second, axis):
        at = x if axis == 0 else y
        first[2].wait_recv()
        first[3].wait_recv()
        second[0].wait_recv()
        second[1].wait_recv()
        for half in range(2):
            stage[:, pl.ds(2 * half, 2)] = part_of(g, axis, at, half)[...] + (raw[half] + summed[half])

    def last_copies(stage, landing, axis, base):
        at = x if axis == 0 else y
        return [
            remote(
                stage.at[:, (at + step) % 4], landing.at[step - 1],
                lat_s.at[base + step - 1], lat_r.at[base + step - 1], *ring_ids(axis, step),
            )
            for step in (1, 2, 3)
        ]

    ring_a = ring_copies(ga, oppa, rawa, suma, 0, 0)
    ring_start(ring_a[0])

    first_gradient((0, 3), slopes, True)

    ring_b = ring_copies(gb, oppb, rawb, sumb, 1, 6)
    ring_start(ring_b[0])
    ring_pass(ga, oppa, *ring_a, 0)
    ring_pass(gb, oppb, *ring_b, 1)
    ring_finish(ga, rawa, suma, stage_a, *ring_a, 0)
    last_a = last_copies(stage_a, lata, 1, 0)
    ring_start(last_a)
    ring_finish(gb, rawb, sumb, stage_b, *ring_b, 1)
    last_b = last_copies(stage_b, latb, 0, 3)
    ring_start(last_b)

    owners = (0, 17)

    def to_owner(layer):
        return remote(sown.at[layer], held.at[m], c_s.at[layer], c_r.at[0], owners[layer], band)

    def hand_over(layer):
        @pl.when(m != owners[layer])
        def _():
            to_owner(layer).start()

        @pl.when(m == owners[layer])
        def _():
            held[m] = sown[layer]

    def keep(layer, total):
        for k in range(9):
            sown[layer, k] = total[k // 3, :, 128 * (k % 3) : 128 * (k % 3) + 128]

    for c in last_a:
        c.wait_recv()
    keep(1, stage_a[:, y] + (lata[0] + (lata[1] + lata[2])))
    hand_over(1)
    for c in last_b:
        c.wait_recv()
    keep(0, stage_b[:, x] + (latb[0] + (latb[1] + latb[2])))
    hand_over(0)

    owner = (m == owners[0]) | (m == owners[1])

    def gram_copy(j):
        return remote(gram_b.at[band], gram_b.at[band], d_s.at[j - 1], d_r.at[0], m, (band + j) % 16)

    def block_copy(k):
        return remote(block, block, e1_s.at[k], e1_r.at[0], 2 * ((depth + FAR_FIRST[k]) % 16) + core, band)

    def finish(layer, alpha):
        totals = [alpha[0:1] * held[0, k] for k in range(9)]
        for q in range(1, 32):
            totals = [v + alpha[q : q + 1] * held[q, k] for k, v in enumerate(totals)]
        for k, v in enumerate(totals):
            t = k if layer == 0 else 3 * (k % 3) + k // 3
            block[pl.ds(t, 8, stride=9), :] = v
        start = pl.multiple_of(72 * band, 8)
        block[...] = fil[layer, pl.ds(start, 72), :] - rates[layer] * block[...]

    @pl.when(owner)
    def _():
        pltpu.make_async_copy(held.at[pl.ds(0, 31)], held.at[pl.ds(0, 31)], c_r.at[0]).wait()
        flat = held.reshape(2304, 128)
        total = jnp.zeros((96, 96), F32)
        for row in range(0, 72, 4):
            lines = [flat[pl.ds(row + q, 32, stride=72), :] for q in range(4)]
            v = jnp.concatenate(thirds(jnp.concatenate(lines, axis=1)), axis=0)
            total = total + nt(v, v)
        total = total[0:32] + total[32:64] + total[64:96]
        total = total[:, 0:32] + total[:, 32:64] + total[:, 64:96]
        gram_b[band] = jnp.concatenate([total[8 * q : 8 * q + 8] for q in range(4)], axis=1)

        @pl.loop(1, 16)
        def _(j):
            gram_copy(j).start()

        pltpu.make_async_copy(gram_b.at[pl.ds(0, 15)], gram_b.at[pl.ds(0, 15)], d_r.at[0]).wait()
        packed = jnp.sum(gram_b[...], axis=0)
        rows = [packed if q == 0 else pltpu.roll(packed, 128 - 32 * q, 1) for q in range(4)]
        gram = jnp.concatenate(rows, axis=0)
        lane = lax.broadcasted_iota(jnp.int32, gram.shape, 1)
        alpha = adasum_weights(jnp.where(lane < 32, gram, 0.0))
        for layer in range(2):
            @pl.when(core == layer)
            def _():
                finish(layer, alpha)

        for k in range(15):
            block_copy(k).start()

    @pl.when(jnp.logical_not(owner))
    def _():
        pltpu.make_async_copy(block, block, e1_r.at[0]).wait()

    start = pl.multiple_of(72 * band, 8)
    place = out.at[core, pl.ds(start, 72)]
    sibling = 2 * depth + 1 - core
    own = pltpu.make_async_copy(block, place, loc_sem.at[0])
    own.start()

    @pl.loop(1, 16)
    def _(j):
        remote(block, place, e2_s.at[j - 1], e2_r.at[j - 1], m, (band + j) % 16).start()

    remote(block, place, f_s.at[0], f_r.at[0], sibling, band).start()

    @pl.loop(1, 16)
    def _(j):
        source = (band + 16 - j) % 16
        there = out.at[core, pl.ds(pl.multiple_of(72 * source, 8), 72)]
        remote(block, there, e2_s.at[j - 1], e2_r.at[j - 1], m, band).wait_recv()
        remote(there, there, f_s.at[j], f_r.at[j], sibling, band).start()

    @pl.loop(0, 16)
    def _(j):
        source = (band + 16 - j) % 16
        there = out.at[1 - core, pl.ds(pl.multiple_of(72 * source, 8), 72)]
        copy = remote(block, there, f_s.at[j], f_r.at[j], sibling, band)
        copy.wait_recv()
        copy.wait_send()

    own.wait()

    @pl.loop(1, 16)
    def _(j):
        remote(block, place, e2_s.at[j - 1], e2_r.at[j - 1], m, band).wait_send()

    @pl.when(band > 0)
    def _():
        halo(xedge, xhalo, 0, True).wait_send()
        halo(yedge, yhalo, 2, True).wait_send()

    @pl.when(band < 15)
    def _():
        halo(xedge, xhalo, 1, False).wait_send()
        halo(yedge, yhalo, 3, False).wait_send()

    for c in (*ring_a[0], *ring_a[1], *ring_b[0], *ring_b[1], *last_a, *last_b):
        c.wait_send()
    for layer in range(2):
        @pl.when(m != owners[layer])
        def _():
            to_owner(layer).wait_send()

    @pl.when(owner)
    def _():
        for k in range(15):
            block_copy(k).wait_send()

        @pl.loop(1, 16)
        def _(j):
            gram_copy(j).wait_send()


def local(images, cotangent, filters, rates):
    dma = pltpu.SemaphoreType.DMA
    hbm = pl.BlockSpec(memory_space=pltpu.HBM)
    vmem = pltpu.VMEM
    new = pl.pallas_call(
        kernel,
        out_shape=jax.ShapeDtypeStruct((2, 1152, 128), F32),
        in_specs=[hbm, hbm, hbm, pl.BlockSpec(memory_space=pltpu.SMEM)],
        out_specs=hbm,
        scratch_shapes=[
            vmem((512, 128), F32), vmem((512, 128), F32), vmem((2, 1152, 128), F32),
            *[vmem((2, 128, 128), F32)] * 4,
            *[vmem((128, 768), BF16)] * 4,
            *[vmem((384, 384), BF16)] * 4,
            vmem((384, 256), F32),
            *[vmem((384, 256), BF16)] * 2,
            *[vmem((3, 4, 4, 8, 384), F32)] * 2,
            *[vmem((2, 3, 2, 8, 384), F32)] * 6,
            *[vmem((3, 4, 8, 384), F32)] * 2,
            *[vmem((3, 3, 8, 384), F32)] * 2,
            vmem((2, 9, 8, 128), F32),
            vmem((32, 9, 8, 128), F32),
            vmem((16, 8, 128), F32),
            vmem((72, 128), F32),
            dma((3,)), dma((4,)), dma((4,)), dma((12,)), dma((12,)), dma((6,)), dma((6,)),
            dma((2,)), dma((1,)), dma((15,)), dma((1,)), dma((15,)), dma((1,)),
            dma((15,)), dma((15,)), dma((16,)), dma((16,)), dma((1,)),
        ],
        compiler_params=pltpu.CompilerParams(
            collective_id=0, has_side_effects=True, vmem_limit_bytes=61 * 1024 * 1024
        ),
        name="adasum_step",
    )(images.reshape(512, 128), cotangent.reshape(512, 128), filters, rates)
    return new[None]


def solution(mesh):
    return jax.shard_map(
        local,
        mesh=mesh,
        in_specs=(P("image", None, "band", None), P("image", None, "band", None), P(), P()),
        out_specs=P("image", None, None, None),
        check_vma=False,
    )
```

```python
import functools

import jax
import jax.numpy as jnp
from jax import lax
from jax.experimental import pallas as pl
from jax.experimental.pallas import tpu as pltpu
from jax.sharding import PartitionSpec as P

MESH = pl.DeviceIdType.MESH
F32 = jnp.float32
BF16 = jnp.bfloat16
HIGH = lax.Precision.HIGHEST


def remote(src, dst, send, recv, image, band):
    return pltpu.make_async_remote_copy(
        src_ref=src,
        dst_ref=dst,
        send_sem=send,
        recv_sem=recv,
        device_id={"image": image, "band": band},
        device_id_type=MESH,
    )


def halves(v):
    hi = v.astype(BF16)
    return hi, (v - hi.astype(F32)).astype(BF16)


def before(v):
    lane = lax.broadcasted_iota(jnp.int32, v.shape, 1)
    return jnp.where(lane == 0, 0.0, pltpu.roll(v, 1, 1))


def after(v):
    lane = lax.broadcasted_iota(jnp.int32, v.shape, 1)
    return jnp.where(lane == 127, 0.0, pltpu.roll(v, 127, 1))


def nn(a, b):
    return lax.dot_general(a, b, (((1,), (0,)), ((), ())), preferred_element_type=F32)


def nt(a, b):
    return lax.dot_general(a, b, (((1,), (1,)), ((), ())), preferred_element_type=F32)


def partner_sum(h, level):
    bit = 1 << level
    if bit >= 8:
        blocks = [h[8 * k : 8 * k + 8] for k in range(4)]
        other = jnp.concatenate([blocks[k ^ (bit // 8)] for k in range(4)], axis=0)
    else:
        blocks = []
        for k in range(4):
            v = h[8 * k : 8 * k + 8]
            r = lax.broadcasted_iota(jnp.int32, v.shape, 0)
            blocks.append(jnp.where((r & bit) == 0, pltpu.roll(v, 8 - bit, 0), pltpu.roll(v, bit, 0)))
        other = jnp.concatenate(blocks, axis=0)
    h = h + other
    lane = lax.broadcasted_iota(jnp.int32, h.shape, 1)
    other = jnp.where((lane & bit) == 0, pltpu.roll(h, 128 - bit, 1), pltpu.roll(h, bit, 1))
    return h + other


def adasum_weights(gram):
    row = lax.broadcasted_iota(jnp.int32, gram.shape, 0)
    lane = lax.broadcasted_iota(jnp.int32, gram.shape, 1)
    alpha = jnp.ones((32, 1), F32)
    for level in range(5):
        own = row == lane
        pair = row == (lane ^ (1 << level))
        sq = jnp.where(own, gram, 0.0)
        inner = jnp.where(pair, gram, 0.0)
        u_col = 1.0 - jnp.sum(inner, axis=1, keepdims=True) / (
            2.0 * (jnp.sum(sq, axis=1, keepdims=True) + 1e-6)
        )
        alpha = alpha * u_col
        if level < 4:
            u_row = 1.0 - jnp.sum(inner, axis=0, keepdims=True) / (
                2.0 * (jnp.sum(sq, axis=0, keepdims=True) + 1e-6)
            )
            gram = partner_sum(gram * u_col * u_row, level)
    return alpha


def thirds(v):
    hi = v.astype(BF16)
    v = v - hi.astype(F32)
    mid = v.astype(BF16)
    return hi, mid, (v - mid.astype(F32)).astype(BF16)


FAR_FIRST = (8, 7, 9, 6, 10, 5, 11, 4, 12, 3, 13, 2, 14, 1, 15)


def kernel(
    img_in, cot_in, fil_in, out,
    img, cot, fil, xedge, yedge, xhalo, yhalo, xh, xl, yh, yl, w1h, w1l, w2h, w2l, z, hh, hl,
    ga, gb, along_x, along_y, sum_x, sum_y, landed, sown,
    held, gram_b, block,
    in_sem, halo_s, halo_r, rs_s, rs_r, last_s, last_r,
    c_s, c_r, d_s, d_r, e1_s, e1_r, e2_s, e2_r, f_s, f_r, loc_sem,
):
    m = lax.axis_index("image")
    band = lax.axis_index("band")
    depth, core = m // 2, m % 2
    y, x = band // 4, band % 4
    scale = 1152.0 ** -0.5

    barrier = pltpu.get_barrier_semaphore()

    def tell(sem, image, place):
        pl.semaphore_signal(
            sem, inc=1, device_id={"image": image, "band": place}, device_id_type=MESH
        )

    @pl.loop(1, 16)
    def _(j):
        tell(barrier, m, (band + j) % 16)

    @pl.loop(1, 32)
    def _(j):
        tell(barrier, (m + j) % 32, band)

    loads = [
        pltpu.make_async_copy(src, dst, in_sem.at[k])
        for k, (src, dst) in enumerate(((img_in, img), (cot_in, cot), (fil_in, fil)))
    ]
    for c in loads:
        c.start()

    for c, field, edge, vh, vl in ((loads[0], img, xedge, xh, xl), (loads[1], cot, yedge, yh, yl)):
        c.wait()
        for r in range(4):
            v = field[pl.ds(r, 128, stride=4), :]
            if r % 3 == 0:
                edge[r // 3] = v
            cols = slice(128 * (r + 1), 128 * (r + 2))
            vh[:, cols], vl[:, cols] = halves(v)

    def halo(edge, landing, k, up):
        if up:
            return remote(edge.at[0], landing.at[1], halo_s.at[k], halo_r.at[k], m, band - 1)
        return remote(edge.at[1], landing.at[0], halo_s.at[k], halo_r.at[k], m, band + 1)

    loads[2].wait()
    for a in range(3):
        for b in range(3):
            rows, cols = slice(128 * b, 128 * b + 128), slice(128 * a, 128 * a + 128)
            w = fil[0, pl.ds(3 * a + b, 128, stride=9), :]
            w1h[rows, cols], w1l[rows, cols] = halves(w.T)
            w2h[rows, cols], w2l[rows, cols] = halves(fil[1, pl.ds(3 * a + b, 128, stride=9), :])

    def columns(ref, pair, offset):
        first, second = (128 * (r + offset) for r in pair)
        return jnp.concatenate([ref[:, first : first + 128], ref[:, second : second + 128]], axis=1)

    def stacked(ref, pair, order):
        return jnp.concatenate([columns(ref, pair, a) for a in order], axis=0)

    def product(wh, wl, hi, lo):
        z[...] = nn(wh[...], hi) + (nn(wh[...], lo) + nn(wl[...], hi))

    def hidden_of(pair):
        product(w1h, w1l, stacked(xh, pair, (0, 1, 2)), stacked(xl, pair, (0, 1, 2)))
        slopes = []
        for q in range(2):
            cols = slice(128 * q, 128 * q + 128)
            pre = scale * (before(z[0:128, cols]) + z[128:256, cols] + after(z[256:384, cols]))
            sig = 1.0 / (1.0 + jnp.exp(-pre))
            hidden = scale * (pre * sig)
            slopes.append((scale * scale) * (sig * (1.0 + pre * (1.0 - sig))))
            for b, v in enumerate((before(hidden), hidden, after(hidden))):
                hh[128 * b : 128 * b + 128, cols], hl[128 * b : 128 * b + 128, cols] = halves(v)
        return slopes

    def second_gradient(pair, add):
        hi, lo = stacked(yh, pair, (2, 1, 0)), stacked(yl, pair, (2, 1, 0))
        for b in range(3):
            rows = slice(128 * b, 128 * b + 128)
            part = nt(hh[rows], hi) + (nt(hh[rows], lo) + nt(hl[rows], hi))
            part = part.reshape(2, 2, 2, 2, 8, 384)
            ga[b] = ga[b] + part if add else part

    def first_gradient(pair, slopes, add):
        product(w2h, w2l, stacked(yh, pair, (2, 1, 0)), stacked(yl, pair, (2, 1, 0)))
        for q in range(2):
            cols = slice(128 * q, 128 * q + 128)
            dpre = (after(z[0:128, cols]) + z[128:256, cols] + before(z[256:384, cols])) * slopes[q]
            for b, v in enumerate((after(dpre), dpre, before(dpre))):
                hh[128 * b : 128 * b + 128, cols], hl[128 * b : 128 * b + 128, cols] = halves(v)
        for a in range(3):
            hi, lo = columns(xh, pair, a), columns(xl, pair, a)
            part = nt(hi, hh[...]) + (nt(hi, hl[...]) + nt(lo, hh[...]))
            part = part.reshape(2, 2, 2, 2, 8, 384)
            gb[a] = gb[a] + part if add else part

    slopes = hidden_of((1, 2))
    second_gradient((1, 2), False)
    first_gradient((1, 2), slopes, False)

    pl.semaphore_wait(barrier, 46)

    @pl.when(band > 0)
    def _():
        halo(xedge, xhalo, 0, True).start()

    @pl.when(band < 15)
    def _():
        halo(xedge, xhalo, 1, False).start()

    @pl.when(band > 0)
    def _():
        halo(yedge, yhalo, 2, True).start()

    @pl.when(band < 15)
    def _():
        halo(yedge, yhalo, 3, False).start()

    @pl.when(band == 0)
    def _():
        xhalo[0] = jnp.zeros((128, 128), F32)
        yhalo[0] = jnp.zeros((128, 128), F32)

    @pl.when(band == 15)
    def _():
        xhalo[1] = jnp.zeros((128, 128), F32)
        yhalo[1] = jnp.zeros((128, 128), F32)

    def halo_arrived(edge, landing, k):
        @pl.when(band < 15)
        def _():
            halo(edge, landing, k, True).wait_recv()

        @pl.when(band > 0)
        def _():
            halo(edge, landing, k + 1, False).wait_recv()

    halo_arrived(xedge, xhalo, 0)
    xh[:, 0:128], xl[:, 0:128] = halves(xhalo[0])
    xh[:, 640:768], xl[:, 640:768] = halves(xhalo[1])
    slopes = hidden_of((0, 3))
    halo_arrived(yedge, yhalo, 2)
    yh[:, 0:128], yl[:, 0:128] = halves(yhalo[0])
    yh[:, 640:768], yl[:, 640:768] = halves(yhalo[1])
    second_gradient((0, 3), True)

    x_half, x_odd, y_half, y_odd = x // 2, x % 2, y // 2, y % 2

    def first_copies(layer, g):
        copies = []
        for step in (1, 2, 3):
            to = (x + step) % 4
            k = 6 * layer + step - 1
            copies.append(
                remote(
                    g.at[:, :, to % 2, to // 2, to % 2], along_x.at[layer, step - 1],
                    rs_s.at[k], rs_r.at[k], m, y * 4 + to,
                )
            )
            to = (y + step) % 4
            copies.append(
                remote(
                    g.at[:, to // 2, to % 2, :, 1 - to % 2], along_y.at[layer, step - 1],
                    rs_s.at[k + 3], rs_r.at[k + 3], m, to * 4 + x,
                )
            )
        return copies

    def last_copies(layer):
        copies = []
        for half in range(2):
            to = 2 * half + x_odd
            slot = (y - to + 3) % 4
            copies.append((to != y, remote(
                sum_x.at[layer, :, half], landed.at[layer, slot],
                last_s.at[4 * layer + half], last_r.at[3 * layer + slot], m, to * 4 + x,
            )))
            to = 2 * half + 1 - y_odd
            slot = (x - to + 3) % 4
            copies.append((to != x, remote(
                sum_y.at[layer, :, half], landed.at[layer, slot],
                last_s.at[4 * layer + 2 + half], last_r.at[3 * layer + slot], m, y * 4 + to,
            )))
        return copies

    def pass_on(layer, g):
        for c in first_copies(layer, g):
            c.wait_recv()
        sum_x[layer] = g[:, :, x_odd, x_half, x_odd] + (
            along_x[layer, 0] + (along_x[layer, 1] + along_x[layer, 2])
        )
        sum_y[layer] = g[:, y_half, y_odd, :, 1 - y_odd] + (
            along_y[layer, 0] + (along_y[layer, 1] + along_y[layer, 2])
        )
        for going, c in last_copies(layer):
            @pl.when(going)
            def _():
                c.start()

    def take(layer):
        for slot in range(3):
            remote(
                landed.at[layer, slot], landed.at[layer, slot],
                last_s.at[0], last_r.at[3 * layer + slot], m, band,
            ).wait_recv()
        own = jnp.where(x_odd == y_odd, sum_x[layer, :, y_half], sum_y[layer, :, x_half])
        total = own + (landed[layer, 0] + (landed[layer, 1] + landed[layer, 2]))
        for k in range(9):
            sown[layer, k] = total[k // 3, :, 128 * (k % 3) : 128 * (k % 3) + 128]

    for c in first_copies(1, ga):
        c.start()
    first_gradient((0, 3), slopes, True)

    for c in first_copies(0, gb):
        c.start()
    pass_on(1, ga)
    pass_on(0, gb)

    owners = (0, 17)

    def to_owner(layer):
        return remote(sown.at[layer], held.at[m], c_s.at[layer], c_r.at[0], owners[layer], band)

    def hand_over(layer):
        @pl.when(m != owners[layer])
        def _():
            to_owner(layer).start()

        @pl.when(m == owners[layer])
        def _():
            held[m] = sown[layer]

    take(1)
    hand_over(1)
    take(0)
    hand_over(0)

    owner = (m == owners[0]) | (m == owners[1])

    def gram_copy(j):
        return remote(gram_b.at[band], gram_b.at[band], d_s.at[j - 1], d_r.at[0], m, (band + j) % 16)

    def block_copy(k):
        return remote(block, block, e1_s.at[k], e1_r.at[0], 2 * ((depth + FAR_FIRST[k]) % 16) + core, band)

    def finish(layer, alpha):
        totals = [alpha[0:1] * held[0, k] for k in range(9)]
        for q in range(1, 32):
            totals = [v + alpha[q : q + 1] * held[q, k] for k, v in enumerate(totals)]
        for k, v in enumerate(totals):
            t = k if layer == 0 else 3 * (k % 3) + k // 3
            block[pl.ds(t, 8, stride=9), :] = v

    @pl.when(owner)
    def _():
        pltpu.make_async_copy(held.at[pl.ds(0, 31)], held.at[pl.ds(0, 31)], c_r.at[0]).wait()
        flat = held.reshape(2304, 128)
        total = jnp.zeros((96, 96), F32)
        for row in range(0, 72, 4):
            lines = [flat[pl.ds(row + q, 32, stride=72), :] for q in range(4)]
            v = jnp.concatenate(thirds(jnp.concatenate(lines, axis=1)), axis=0)
            total = total + nt(v, v)
        total = total[0:32] + total[32:64] + total[64:96]
        total = total[:, 0:32] + total[:, 32:64] + total[:, 64:96]
        gram_b[band] = jnp.concatenate([total[8 * q : 8 * q + 8] for q in range(4)], axis=1)

        @pl.loop(1, 16)
        def _(j):
            gram_copy(j).start()

        pltpu.make_async_copy(gram_b.at[pl.ds(0, 15)], gram_b.at[pl.ds(0, 15)], d_r.at[0]).wait()
        packed = jnp.sum(gram_b[...], axis=0)
        rows = [packed if q == 0 else pltpu.roll(packed, 128 - 32 * q, 1) for q in range(4)]
        gram = jnp.concatenate(rows, axis=0)
        lane = lax.broadcasted_iota(jnp.int32, gram.shape, 1)
        alpha = adasum_weights(jnp.where(lane < 32, gram, 0.0))
        for layer in range(2):
            @pl.when(core == layer)
            def _():
                finish(layer, alpha)

        for k in range(15):
            block_copy(k).start()

    @pl.when(jnp.logical_not(owner))
    def _():
        pltpu.make_async_copy(block, block, e1_r.at[0]).wait()

    start = pl.multiple_of(72 * band, 8)
    place = out.at[core, pl.ds(start, 72)]
    sibling = 2 * depth + 1 - core
    own = pltpu.make_async_copy(block, place, loc_sem.at[0])
    own.start()

    @pl.loop(1, 16)
    def _(j):
        remote(block, place, e2_s.at[j - 1], e2_r.at[j - 1], m, (band + j) % 16).start()

    remote(block, place, f_s.at[0], f_r.at[0], sibling, band).start()

    @pl.loop(1, 16)
    def _(j):
        source = (band + 16 - j) % 16
        there = out.at[core, pl.ds(pl.multiple_of(72 * source, 8), 72)]
        remote(block, there, e2_s.at[j - 1], e2_r.at[j - 1], m, band).wait_recv()
        remote(there, there, f_s.at[j], f_r.at[j], sibling, band).start()

    @pl.loop(0, 16)
    def _(j):
        source = (band + 16 - j) % 16
        there = out.at[1 - core, pl.ds(pl.multiple_of(72 * source, 8), 72)]
        copy = remote(block, there, f_s.at[j], f_r.at[j], sibling, band)
        copy.wait_recv()
        copy.wait_send()

    own.wait()

    @pl.loop(1, 16)
    def _(j):
        remote(block, place, e2_s.at[j - 1], e2_r.at[j - 1], m, band).wait_send()

    @pl.when(band > 0)
    def _():
        halo(xedge, xhalo, 0, True).wait_send()
        halo(yedge, yhalo, 2, True).wait_send()

    @pl.when(band < 15)
    def _():
        halo(xedge, xhalo, 1, False).wait_send()
        halo(yedge, yhalo, 3, False).wait_send()

    for layer, g in ((0, gb), (1, ga)):
        for c in first_copies(layer, g):
            c.wait_send()
        for going, c in last_copies(layer):
            @pl.when(going)
            def _():
                c.wait_send()
    for layer in range(2):
        @pl.when(m != owners[layer])
        def _():
            to_owner(layer).wait_send()

    @pl.when(owner)
    def _():
        for k in range(15):
            block_copy(k).wait_send()

        @pl.loop(1, 16)
        def _(j):
            gram_copy(j).wait_send()


def local(images, cotangent, filters, rates):
    dma = pltpu.SemaphoreType.DMA
    hbm = pl.BlockSpec(memory_space=pltpu.HBM)
    vmem = pltpu.VMEM
    merged = pl.pallas_call(
        kernel,
        out_shape=jax.ShapeDtypeStruct((2, 1152, 128), F32),
        in_specs=[hbm, hbm, hbm],
        out_specs=hbm,
        scratch_shapes=[
            vmem((512, 128), F32), vmem((512, 128), F32), vmem((2, 1152, 128), F32),
            *[vmem((2, 128, 128), F32)] * 4,
            *[vmem((128, 768), BF16)] * 4,
            *[vmem((384, 384), BF16)] * 4,
            vmem((384, 256), F32),
            *[vmem((384, 256), BF16)] * 2,
            *[vmem((3, 2, 2, 2, 2, 8, 384), F32)] * 2,
            *[vmem((2, 3, 3, 2, 8, 384), F32)] * 2,
            *[vmem((2, 3, 2, 8, 384), F32)] * 2,
            vmem((2, 3, 3, 8, 384), F32),
            vmem((2, 9, 8, 128), F32),
            vmem((32, 9, 8, 128), F32),
            vmem((16, 8, 128), F32),
            vmem((72, 128), F32),
            dma((3,)), dma((4,)), dma((4,)),
            dma((12,)), dma((12,)), dma((8,)), dma((6,)),
            dma((2,)), dma((1,)), dma((15,)), dma((1,)), dma((15,)), dma((1,)),
            dma((15,)), dma((15,)), dma((16,)), dma((16,)), dma((1,)),
        ],
        compiler_params=pltpu.CompilerParams(
            collective_id=0, has_side_effects=True, vmem_limit_bytes=61 * 1024 * 1024
        ),
        name="adasum_step",
    )(images.reshape(512, 128), cotangent.reshape(512, 128), filters)
    return (filters - rates[:, None, None] * merged)[None]


def solution(mesh):
    return jax.shard_map(
        local,
        mesh=mesh,
        in_specs=(P("image", None, "band", None), P("image", None, "band", None), P(), P()),
        out_specs=P("image", None, None, None),
        check_vma=False,
    )
```

```python
import functools

import jax
import jax.numpy as jnp
from jax import lax
from jax.experimental import pallas as pl
from jax.experimental.pallas import tpu as pltpu
from jax.sharding import PartitionSpec as P

MESH = pl.DeviceIdType.MESH
F32 = jnp.float32
BF16 = jnp.bfloat16
HIGH = lax.Precision.HIGHEST


def remote(src, dst, send, recv, image, band):
    return pltpu.make_async_remote_copy(
        src_ref=src,
        dst_ref=dst,
        send_sem=send,
        recv_sem=recv,
        device_id={"image": image, "band": band},
        device_id_type=MESH,
    )


def halves(v):
    hi = v.astype(BF16)
    return hi, (v - hi.astype(F32)).astype(BF16)


def before(v):
    lane = lax.broadcasted_iota(jnp.int32, v.shape, 1)
    return jnp.where(lane == 0, 0.0, pltpu.roll(v, 1, 1))


def after(v):
    lane = lax.broadcasted_iota(jnp.int32, v.shape, 1)
    return jnp.where(lane == 127, 0.0, pltpu.roll(v, 127, 1))


def nn(a, b):
    return lax.dot_general(a, b, (((1,), (0,)), ((), ())), preferred_element_type=F32)


def nt(a, b):
    return lax.dot_general(a, b, (((1,), (1,)), ((), ())), preferred_element_type=F32)


def partner_sum(h, level):
    bit = 1 << level
    if bit >= 8:
        blocks = [h[8 * k : 8 * k + 8] for k in range(4)]
        other = jnp.concatenate([blocks[k ^ (bit // 8)] for k in range(4)], axis=0)
    else:
        blocks = []
        for k in range(4):
            v = h[8 * k : 8 * k + 8]
            r = lax.broadcasted_iota(jnp.int32, v.shape, 0)
            blocks.append(jnp.where((r & bit) == 0, pltpu.roll(v, 8 - bit, 0), pltpu.roll(v, bit, 0)))
        other = jnp.concatenate(blocks, axis=0)
    h = h + other
    lane = lax.broadcasted_iota(jnp.int32, h.shape, 1)
    other = jnp.where((lane & bit) == 0, pltpu.roll(h, 128 - bit, 1), pltpu.roll(h, bit, 1))
    return h + other


def adasum_weights(gram):
    row = lax.broadcasted_iota(jnp.int32, gram.shape, 0)
    lane = lax.broadcasted_iota(jnp.int32, gram.shape, 1)
    alpha = jnp.ones((32, 1), F32)
    for level in range(5):
        own = row == lane
        pair = row == (lane ^ (1 << level))
        sq = jnp.where(own, gram, 0.0)
        inner = jnp.where(pair, gram, 0.0)
        u_col = 1.0 - jnp.sum(inner, axis=1, keepdims=True) / (
            2.0 * (jnp.sum(sq, axis=1, keepdims=True) + 1e-6)
        )
        alpha = alpha * u_col
        if level < 4:
            u_row = 1.0 - jnp.sum(inner, axis=0, keepdims=True) / (
                2.0 * (jnp.sum(sq, axis=0, keepdims=True) + 1e-6)
            )
            gram = partner_sum(gram * u_col * u_row, level)
    return alpha


def thirds(v):
    hi = v.astype(BF16)
    v = v - hi.astype(F32)
    mid = v.astype(BF16)
    return hi, mid, (v - mid.astype(F32)).astype(BF16)


OWNERS = (2, 9)
ORDER = (0, 1, 2, 3, 4, 15, 5, 14, 6, 13, 7, 12, 8, 11, 9, 10)


def kernel(
    img_in, cot_in, fil_in, out,
    img, cot, fil, xedge, yedge, xhalo, yhalo, xh, xl, yh, yl, w1h, w1l, w2h, w2l, z, hh, hl,
    ga, gb, along_x, along_y, sum_x, sum_y, landed, sown,
    held, gram_b, block,
    in_sem, halo_s, halo_r, rs_s, rs_r, last_s, last_r,
    c_s, c_r, d_s, d_r, e1_s, e1_r, e2_s, e2_r, f_s, f_r, loc_sem,
):
    m = lax.axis_index("image")
    band = lax.axis_index("band")
    depth, core = m // 2, m % 2
    y, x = band // 4, band % 4
    scale = 1152.0 ** -0.5

    barrier = pltpu.get_barrier_semaphore()

    def tell(sem, image, place):
        pl.semaphore_signal(
            sem, inc=1, device_id={"image": image, "band": place}, device_id_type=MESH
        )

    sibling = m + 1 - 2 * core
    owner = (m == OWNERS[0]) | (m == OWNERS[1])
    beside_owner = (sibling == OWNERS[0]) | (sibling == OWNERS[1])

    @pl.loop(1, 16)
    def _(j):
        tell(barrier, m, (band + j) % 16)

    @pl.when(owner)
    def _():
        @pl.loop(1, 32)
        def _(j):
            tell(barrier, (m + j) % 32, band)

    @pl.when(jnp.logical_not(owner))
    def _():
        tell(barrier, sibling, band)

    loads = [
        pltpu.make_async_copy(src, dst, in_sem.at[k])
        for k, (src, dst) in enumerate(((img_in, img), (cot_in, cot), (fil_in, fil)))
    ]
    for c in loads:
        c.start()

    for c, field, edge, vh, vl in ((loads[0], img, xedge, xh, xl), (loads[1], cot, yedge, yh, yl)):
        c.wait()
        for r in range(4):
            v = field[pl.ds(r, 128, stride=4), :]
            if r % 3 == 0:
                edge[r // 3] = v
            cols = slice(128 * (r + 1), 128 * (r + 2))
            vh[:, cols], vl[:, cols] = halves(v)

    def halo(edge, landing, k, up):
        if up:
            return remote(edge.at[0], landing.at[1], halo_s.at[k], halo_r.at[k], m, band - 1)
        return remote(edge.at[1], landing.at[0], halo_s.at[k], halo_r.at[k], m, band + 1)

    @pl.when(owner | beside_owner)
    def _():
        pl.semaphore_wait(barrier, 17)

    @pl.when(jnp.logical_not(owner | beside_owner))
    def _():
        pl.semaphore_wait(barrier, 18)


    @pl.when(band > 0)
    def _():
        halo(xedge, xhalo, 0, True).start()

    @pl.when(band < 15)
    def _():
        halo(xedge, xhalo, 1, False).start()

    @pl.when(band > 0)
    def _():
        halo(yedge, yhalo, 2, True).start()

    @pl.when(band < 15)
    def _():
        halo(yedge, yhalo, 3, False).start()

    loads[2].wait()
    for a in range(3):
        for b in range(3):
            rows, cols = slice(128 * b, 128 * b + 128), slice(128 * a, 128 * a + 128)
            w = fil[0, pl.ds(3 * a + b, 128, stride=9), :]
            w1h[rows, cols], w1l[rows, cols] = halves(w.T)
            w2h[rows, cols], w2l[rows, cols] = halves(fil[1, pl.ds(3 * a + b, 128, stride=9), :])

    def columns(ref, pair, offset):
        first, second = (128 * (r + offset) for r in pair)
        return jnp.concatenate([ref[:, first : first + 128], ref[:, second : second + 128]], axis=1)

    def stacked(ref, pair, order):
        return jnp.concatenate([columns(ref, pair, a) for a in order], axis=0)

    def product(wh, wl, hi, lo):
        z[...] = nn(wh[...], hi) + (nn(wh[...], lo) + nn(wl[...], hi))

    def hidden_of(pair):
        product(w1h, w1l, stacked(xh, pair, (0, 1, 2)), stacked(xl, pair, (0, 1, 2)))
        slopes = []
        for q in range(2):
            cols = slice(128 * q, 128 * q + 128)
            pre = scale * (before(z[0:128, cols]) + z[128:256, cols] + after(z[256:384, cols]))
            sig = 1.0 / (1.0 + jnp.exp(-pre))
            hidden = scale * (pre * sig)
            slopes.append((scale * scale) * (sig * (1.0 + pre * (1.0 - sig))))
            for b, v in enumerate((before(hidden), hidden, after(hidden))):
                hh[128 * b : 128 * b + 128, cols], hl[128 * b : 128 * b + 128, cols] = halves(v)
        return slopes

    def second_gradient(pair, add):
        hi, lo = stacked(yh, pair, (2, 1, 0)), stacked(yl, pair, (2, 1, 0))
        for b in range(3):
            rows = slice(128 * b, 128 * b + 128)
            part = nt(hh[rows], hi) + (nt(hh[rows], lo) + nt(hl[rows], hi))
            part = part.reshape(2, 2, 2, 2, 8, 384)
            ga[b] = ga[b] + part if add else part

    def first_gradient(pair, slopes, add):
        product(w2h, w2l, stacked(yh, pair, (2, 1, 0)), stacked(yl, pair, (2, 1, 0)))
        for q in range(2):
            cols = slice(128 * q, 128 * q + 128)
            dpre = (after(z[0:128, cols]) + z[128:256, cols] + before(z[256:384, cols])) * slopes[q]
            for b, v in enumerate((after(dpre), dpre, before(dpre))):
                hh[128 * b : 128 * b + 128, cols], hl[128 * b : 128 * b + 128, cols] = halves(v)
        for a in range(3):
            hi, lo = columns(xh, pair, a), columns(xl, pair, a)
            part = nt(hi, hh[...]) + (nt(hi, hl[...]) + nt(lo, hh[...]))
            part = part.reshape(2, 2, 2, 2, 8, 384)
            gb[a] = gb[a] + part if add else part

    slopes = hidden_of((1, 2))
    second_gradient((1, 2), False)
    first_gradient((1, 2), slopes, False)

    @pl.when(band == 0)
    def _():
        xhalo[0] = jnp.zeros((128, 128), F32)
        yhalo[0] = jnp.zeros((128, 128), F32)

    @pl.when(band == 15)
    def _():
        xhalo[1] = jnp.zeros((128, 128), F32)
        yhalo[1] = jnp.zeros((128, 128), F32)

    def halo_arrived(edge, landing, k):
        @pl.when(band < 15)
        def _():
            halo(edge, landing, k, True).wait_recv()

        @pl.when(band > 0)
        def _():
            halo(edge, landing, k + 1, False).wait_recv()

    halo_arrived(xedge, xhalo, 0)
    xh[:, 0:128], xl[:, 0:128] = halves(xhalo[0])
    xh[:, 640:768], xl[:, 640:768] = halves(xhalo[1])
    slopes = hidden_of((0, 3))
    halo_arrived(yedge, yhalo, 2)
    yh[:, 0:128], yl[:, 0:128] = halves(yhalo[0])
    yh[:, 640:768], yl[:, 640:768] = halves(yhalo[1])
    second_gradient((0, 3), True)

    x_half, x_odd, y_half, y_odd = x // 2, x % 2, y // 2, y % 2

    def first_copies(layer, g):
        copies = []
        for step in (1, 2, 3):
            to = (x + step) % 4
            k = 6 * layer + step - 1
            copies.append(
                remote(
                    g.at[:, :, to % 2, to // 2, to % 2], along_x.at[layer, step - 1],
                    rs_s.at[k], rs_r.at[k], m, y * 4 + to,
                )
            )
            to = (y + step) % 4
            copies.append(
                remote(
                    g.at[:, to // 2, to % 2, :, 1 - to % 2], along_y.at[layer, step - 1],
                    rs_s.at[k + 3], rs_r.at[k + 3], m, to * 4 + x,
                )
            )
        return copies

    def last_copies(layer):
        copies = []
        for half in range(2):
            to = 2 * half + x_odd
            slot = (y - to + 3) % 4
            copies.append((to != y, remote(
                sum_x.at[layer, :, half], landed.at[layer, slot],
                last_s.at[4 * layer + half], last_r.at[3 * layer + slot], m, to * 4 + x,
            )))
            to = 2 * half + 1 - y_odd
            slot = (x - to + 3) % 4
            copies.append((to != x, remote(
                sum_y.at[layer, :, half], landed.at[layer, slot],
                last_s.at[4 * layer + 2 + half], last_r.at[3 * layer + slot], m, y * 4 + to,
            )))
        return copies

    def pass_on(layer, g):
        for c in first_copies(layer, g):
            c.wait_recv()
        sum_x[layer] = g[:, :, x_odd, x_half, x_odd] + (
            along_x[layer, 0] + (along_x[layer, 1] + along_x[layer, 2])
        )
        sum_y[layer] = g[:, y_half, y_odd, :, 1 - y_odd] + (
            along_y[layer, 0] + (along_y[layer, 1] + along_y[layer, 2])
        )
        for going, c in last_copies(layer):
            @pl.when(going)
            def _():
                c.start()

    def take(layer):
        for slot in range(3):
            remote(
                landed.at[layer, slot], landed.at[layer, slot],
                last_s.at[0], last_r.at[3 * layer + slot], m, band,
            ).wait_recv()
        own = jnp.where(x_odd == y_odd, sum_x[layer, :, y_half], sum_y[layer, :, x_half])
        total = own + (landed[layer, 0] + (landed[layer, 1] + landed[layer, 2]))
        for k in range(9):
            sown[layer, k] = total[k // 3, :, 128 * (k % 3) : 128 * (k % 3) + 128]

    for c in first_copies(1, ga):
        c.start()
    first_gradient((0, 3), slopes, True)

    for c in first_copies(0, gb):
        c.start()
    pass_on(1, ga)
    pass_on(0, gb)

    def to_owner(layer):
        return remote(sown.at[layer], held.at[m], c_s.at[layer], c_r.at[0], OWNERS[layer], band)

    def hand_over(layer):
        @pl.when(m != OWNERS[layer])
        def _():
            to_owner(layer).start()

        @pl.when(m == OWNERS[layer])
        def _():
            held[m] = sown[layer]

    take(1)
    hand_over(1)
    take(0)
    hand_over(0)

    def gram_copy(j):
        return remote(gram_b.at[band], gram_b.at[band], d_s.at[j - 1], d_r.at[0], m, (band + j) % 16)

    def block_copy(to):
        return remote(block, block, e1_s.at[to], e1_r.at[0], 2 * to + core, band)

    def finish(layer, alpha):
        totals = [alpha[0:1] * held[0, k] for k in range(9)]
        for q in range(1, 32):
            totals = [v + alpha[q : q + 1] * held[q, k] for k, v in enumerate(totals)]
        for k, v in enumerate(totals):
            t = k if layer == 0 else 3 * (k % 3) + k // 3
            block[pl.ds(t, 8, stride=9), :] = v

    @pl.when(owner)
    def _():
        pltpu.make_async_copy(held.at[pl.ds(0, 31)], held.at[pl.ds(0, 31)], c_r.at[0]).wait()
        flat = held.reshape(2304, 128)
        total = jnp.zeros((96, 96), F32)
        for row in range(0, 72, 4):
            lines = [flat[pl.ds(row + q, 32, stride=72), :] for q in range(4)]
            v = jnp.concatenate(thirds(jnp.concatenate(lines, axis=1)), axis=0)
            total = total + nt(v, v)
        total = total[0:32] + total[32:64] + total[64:96]
        total = total[:, 0:32] + total[:, 32:64] + total[:, 64:96]
        gram_b[band] = jnp.concatenate([total[8 * q : 8 * q + 8] for q in range(4)], axis=1)

        @pl.loop(1, 16)
        def _(j):
            gram_copy(j).start()

        pltpu.make_async_copy(gram_b.at[pl.ds(0, 15)], gram_b.at[pl.ds(0, 15)], d_r.at[0]).wait()
        packed = jnp.sum(gram_b[...], axis=0)
        rows = [packed if q == 0 else pltpu.roll(packed, 128 - 32 * q, 1) for q in range(4)]
        gram = jnp.concatenate(rows, axis=0)
        lane = lax.broadcasted_iota(jnp.int32, gram.shape, 1)
        alpha = adasum_weights(jnp.where(lane < 32, gram, 0.0))
        for layer in range(2):
            @pl.when(core == layer)
            def _():
                finish(layer, alpha)

        for to in ORDER:
            @pl.when(to != depth)
            def _():
                block_copy(to).start()

    @pl.when(jnp.logical_not(owner))
    def _():
        pltpu.make_async_copy(block, block, e1_r.at[0]).wait()

    start = pl.multiple_of(72 * band, 8)
    place = out.at[core, pl.ds(start, 72)]
    own = pltpu.make_async_copy(block, place, loc_sem.at[0])
    own.start()

    @pl.loop(1, 16)
    def _(j):
        remote(block, place, e2_s.at[j - 1], e2_r.at[j - 1], m, (band + j) % 16).start()

    remote(block, place, f_s.at[0], f_r.at[0], sibling, band).start()

    @pl.loop(1, 16)
    def _(j):
        source = (band + 16 - j) % 16
        there = out.at[core, pl.ds(pl.multiple_of(72 * source, 8), 72)]
        remote(block, there, e2_s.at[j - 1], e2_r.at[j - 1], m, band).wait_recv()
        remote(there, there, f_s.at[j], f_r.at[j], sibling, band).start()

    @pl.loop(0, 16)
    def _(j):
        source = (band + 16 - j) % 16
        there = out.at[1 - core, pl.ds(pl.multiple_of(72 * source, 8), 72)]
        copy = remote(block, there, f_s.at[j], f_r.at[j], sibling, band)
        copy.wait_recv()
        copy.wait_send()

    own.wait()

    @pl.loop(1, 16)
    def _(j):
        remote(block, place, e2_s.at[j - 1], e2_r.at[j - 1], m, band).wait_send()

    @pl.when(band > 0)
    def _():
        halo(xedge, xhalo, 0, True).wait_send()
        halo(yedge, yhalo, 2, True).wait_send()

    @pl.when(band < 15)
    def _():
        halo(xedge, xhalo, 1, False).wait_send()
        halo(yedge, yhalo, 3, False).wait_send()

    for layer, g in ((0, gb), (1, ga)):
        for c in first_copies(layer, g):
            c.wait_send()
        for going, c in last_copies(layer):
            @pl.when(going)
            def _():
                c.wait_send()
    for layer in range(2):
        @pl.when(m != OWNERS[layer])
        def _():
            to_owner(layer).wait_send()

    @pl.when(owner)
    def _():
        for to in ORDER:
            @pl.when(to != depth)
            def _():
                block_copy(to).wait_send()

        @pl.loop(1, 16)
        def _(j):
            gram_copy(j).wait_send()


def local(images, cotangent, filters, rates):
    dma = pltpu.SemaphoreType.DMA
    hbm = pl.BlockSpec(memory_space=pltpu.HBM)
    vmem = pltpu.VMEM
    merged = pl.pallas_call(
        kernel,
        out_shape=jax.ShapeDtypeStruct((2, 1152, 128), F32),
        in_specs=[hbm, hbm, hbm],
        out_specs=hbm,
        scratch_shapes=[
            vmem((512, 128), F32), vmem((512, 128), F32), vmem((2, 1152, 128), F32),
            *[vmem((2, 128, 128), F32)] * 4,
            *[vmem((128, 768), BF16)] * 4,
            *[vmem((384, 384), BF16)] * 4,
            vmem((384, 256), F32),
            *[vmem((384, 256), BF16)] * 2,
            *[vmem((3, 2, 2, 2, 2, 8, 384), F32)] * 2,
            *[vmem((2, 3, 3, 2, 8, 384), F32)] * 2,
            *[vmem((2, 3, 2, 8, 384), F32)] * 2,
            vmem((2, 3, 3, 8, 384), F32),
            vmem((2, 9, 8, 128), F32),
            vmem((32, 9, 8, 128), F32),
            vmem((16, 8, 128), F32),
            vmem((72, 128), F32),
            dma((3,)), dma((4,)), dma((4,)),
            dma((12,)), dma((12,)), dma((8,)), dma((6,)),
            dma((2,)), dma((1,)), dma((15,)), dma((1,)), dma((16,)), dma((1,)),
            dma((15,)), dma((15,)), dma((16,)), dma((16,)), dma((1,)),
        ],
        compiler_params=pltpu.CompilerParams(
            collective_id=0, has_side_effects=True, vmem_limit_bytes=61 * 1024 * 1024
        ),
        name="adasum_step",
    )(images.reshape(512, 128), cotangent.reshape(512, 128), filters)
    return (filters - rates[:, None, None] * merged)[None]


def solution(mesh):
    return jax.shard_map(
        local,
        mesh=mesh,
        in_specs=(P("image", None, "band", None), P("image", None, "band", None), P(), P()),
        out_specs=P("image", None, None, None),
        check_vma=False,
    )
```

```python
import functools

import jax
import jax.numpy as jnp
from jax import lax
from jax.experimental import pallas as pl
from jax.experimental.pallas import tpu as pltpu
from jax.sharding import PartitionSpec as P

MESH = pl.DeviceIdType.MESH
F32 = jnp.float32
BF16 = jnp.bfloat16
HIGH = lax.Precision.HIGHEST


def remote(src, dst, send, recv, image, band):
    return pltpu.make_async_remote_copy(
        src_ref=src,
        dst_ref=dst,
        send_sem=send,
        recv_sem=recv,
        device_id={"image": image, "band": band},
        device_id_type=MESH,
    )


def halves(v):
    hi = v.astype(BF16)
    return hi, (v - hi.astype(F32)).astype(BF16)


def before(v):
    lane = lax.broadcasted_iota(jnp.int32, v.shape, 1)
    return jnp.where(lane == 0, 0.0, pltpu.roll(v, 1, 1))


def after(v):
    lane = lax.broadcasted_iota(jnp.int32, v.shape, 1)
    return jnp.where(lane == 127, 0.0, pltpu.roll(v, 127, 1))


def nn(a, b):
    return lax.dot_general(a, b, (((1,), (0,)), ((), ())), preferred_element_type=F32)


def nt(a, b):
    return lax.dot_general(a, b, (((1,), (1,)), ((), ())), preferred_element_type=F32)


def partner_sum(h, level):
    bit = 1 << level
    if bit >= 8:
        blocks = [h[8 * k : 8 * k + 8] for k in range(4)]
        other = jnp.concatenate([blocks[k ^ (bit // 8)] for k in range(4)], axis=0)
    else:
        blocks = []
        for k in range(4):
            v = h[8 * k : 8 * k + 8]
            r = lax.broadcasted_iota(jnp.int32, v.shape, 0)
            blocks.append(jnp.where((r & bit) == 0, pltpu.roll(v, 8 - bit, 0), pltpu.roll(v, bit, 0)))
        other = jnp.concatenate(blocks, axis=0)
    h = h + other
    lane = lax.broadcasted_iota(jnp.int32, h.shape, 1)
    other = jnp.where((lane & bit) == 0, pltpu.roll(h, 128 - bit, 1), pltpu.roll(h, bit, 1))
    return h + other


def adasum_weights(gram):
    row = lax.broadcasted_iota(jnp.int32, gram.shape, 0)
    lane = lax.broadcasted_iota(jnp.int32, gram.shape, 1)
    alpha = jnp.ones((32, 1), F32)
    for level in range(5):
        own = row == lane
        pair = row == (lane ^ (1 << level))
        sq = jnp.where(own, gram, 0.0)
        inner = jnp.where(pair, gram, 0.0)
        u_col = 1.0 - jnp.sum(inner, axis=1, keepdims=True) / (
            2.0 * (jnp.sum(sq, axis=1, keepdims=True) + 1e-6)
        )
        alpha = alpha * u_col
        if level < 4:
            u_row = 1.0 - jnp.sum(inner, axis=0, keepdims=True) / (
                2.0 * (jnp.sum(sq, axis=0, keepdims=True) + 1e-6)
            )
            gram = partner_sum(gram * u_col * u_row, level)
    return alpha


def thirds(v):
    hi = v.astype(BF16)
    v = v - hi.astype(F32)
    mid = v.astype(BF16)
    return hi, mid, (v - mid.astype(F32)).astype(BF16)


OWNERS = (4, 7)
ORDER = (0, 1, 2, 3, 4, 15, 5, 14, 6, 13, 7, 12, 8, 11, 9, 10)


def kernel(
    img_in, cot_in, fil_in, out,
    img, cot, fil, xedge, yedge, xhalo, yhalo, xh, xl, yh, yl, w1h, w1l, w2h, w2l, z, hh, hl,
    ga, gb, along_x, along_y, sum_x, sum_y, landed, sown,
    held, gram_b, block,
    in_sem, halo_s, halo_r, rs_s, rs_r, last_s, last_r,
    c_s, c_r, d_s, d_r, e1_s, e1_r, e2_s, e2_r, f_s, f_r, loc_sem,
):
    m = lax.axis_index("image")
    band = lax.axis_index("band")
    depth, core = m // 2, m % 2
    y, x = band // 4, band % 4
    scale = 1152.0 ** -0.5

    barrier = pltpu.get_barrier_semaphore()

    def tell(sem, image, place):
        pl.semaphore_signal(
            sem, inc=1, device_id={"image": image, "band": place}, device_id_type=MESH
        )

    sibling = m + 1 - 2 * core
    owner = (m == OWNERS[0]) | (m == OWNERS[1])
    beside_owner = (sibling == OWNERS[0]) | (sibling == OWNERS[1])

    @pl.loop(1, 16)
    def _(j):
        tell(barrier, m, (band + j) % 16)

    @pl.when(owner)
    def _():
        @pl.loop(1, 32)
        def _(j):
            tell(barrier, (m + j) % 32, band)

    @pl.when(jnp.logical_not(owner))
    def _():
        tell(barrier, sibling, band)

    loads = [
        pltpu.make_async_copy(src, dst, in_sem.at[k])
        for k, (src, dst) in enumerate(((img_in, img), (cot_in, cot), (fil_in, fil)))
    ]
    for c in loads:
        c.start()

    for c, field, edge, vh, vl in ((loads[0], img, xedge, xh, xl), (loads[1], cot, yedge, yh, yl)):
        c.wait()
        for r in range(4):
            v = field[pl.ds(r, 128, stride=4), :]
            if r % 3 == 0:
                edge[r // 3] = v
            cols = slice(128 * (r + 1), 128 * (r + 2))
            vh[:, cols], vl[:, cols] = halves(v)

    def halo(edge, landing, k, up):
        if up:
            return remote(edge.at[0], landing.at[1], halo_s.at[k], halo_r.at[k], m, band - 1)
        return remote(edge.at[1], landing.at[0], halo_s.at[k], halo_r.at[k], m, band + 1)

    @pl.when(owner | beside_owner)
    def _():
        pl.semaphore_wait(barrier, 17)

    @pl.when(jnp.logical_not(owner | beside_owner))
    def _():
        pl.semaphore_wait(barrier, 18)


    @pl.when(band > 0)
    def _():
        halo(xedge, xhalo, 0, True).start()

    @pl.when(band < 15)
    def _():
        halo(xedge, xhalo, 1, False).start()

    @pl.when(band > 0)
    def _():
        halo(yedge, yhalo, 2, True).start()

    @pl.when(band < 15)
    def _():
        halo(yedge, yhalo, 3, False).start()

    loads[2].wait()
    for a in range(3):
        for b in range(3):
            rows, cols = slice(128 * b, 128 * b + 128), slice(128 * a, 128 * a + 128)
            w = fil[0, pl.ds(3 * a + b, 128, stride=9), :]
            w1h[rows, cols], w1l[rows, cols] = halves(w.T)
            w2h[rows, cols], w2l[rows, cols] = halves(fil[1, pl.ds(3 * a + b, 128, stride=9), :])

    def columns(ref, pair, offset):
        first, second = (128 * (r + offset) for r in pair)
        return jnp.concatenate([ref[:, first : first + 128], ref[:, second : second + 128]], axis=1)

    def stacked(ref, pair, order):
        return jnp.concatenate([columns(ref, pair, a) for a in order], axis=0)

    def product(wh, wl, hi, lo):
        z[...] = nn(wh[...], hi) + (nn(wh[...], lo) + nn(wl[...], hi))

    def hidden_of(pair):
        product(w1h, w1l, stacked(xh, pair, (0, 1, 2)), stacked(xl, pair, (0, 1, 2)))
        slopes = []
        for q in range(2):
            cols = slice(128 * q, 128 * q + 128)
            pre = scale * (before(z[0:128, cols]) + z[128:256, cols] + after(z[256:384, cols]))
            sig = 1.0 / (1.0 + jnp.exp(-pre))
            hidden = scale * (pre * sig)
            slopes.append((scale * scale) * (sig * (1.0 + pre * (1.0 - sig))))
            for b, v in enumerate((before(hidden), hidden, after(hidden))):
                hh[128 * b : 128 * b + 128, cols], hl[128 * b : 128 * b + 128, cols] = halves(v)
        return slopes

    def second_gradient(pair, add):
        hi, lo = stacked(yh, pair, (2, 1, 0)), stacked(yl, pair, (2, 1, 0))
        for b in range(3):
            rows = slice(128 * b, 128 * b + 128)
            part = nt(hh[rows], hi) + (nt(hh[rows], lo) + nt(hl[rows], hi))
            part = part.reshape(2, 2, 2, 2, 8, 384)
            ga[b] = ga[b] + part if add else part

    def first_gradient(pair, slopes, add):
        product(w2h, w2l, stacked(yh, pair, (2, 1, 0)), stacked(yl, pair, (2, 1, 0)))
        for q in range(2):
            cols = slice(128 * q, 128 * q + 128)
            dpre = (after(z[0:128, cols]) + z[128:256, cols] + before(z[256:384, cols])) * slopes[q]
            for b, v in enumerate((after(dpre), dpre, before(dpre))):
                hh[128 * b : 128 * b + 128, cols], hl[128 * b : 128 * b + 128, cols] = halves(v)
        for a in range(3):
            hi, lo = columns(xh, pair, a), columns(xl, pair, a)
            part = nt(hi, hh[...]) + (nt(hi, hl[...]) + nt(lo, hh[...]))
            part = part.reshape(2, 2, 2, 2, 8, 384)
            gb[a] = gb[a] + part if add else part

    slopes = hidden_of((1, 2))
    second_gradient((1, 2), False)
    first_gradient((1, 2), slopes, False)

    @pl.when(band == 0)
    def _():
        xhalo[0] = jnp.zeros((128, 128), F32)
        yhalo[0] = jnp.zeros((128, 128), F32)

    @pl.when(band == 15)
    def _():
        xhalo[1] = jnp.zeros((128, 128), F32)
        yhalo[1] = jnp.zeros((128, 128), F32)

    def halo_arrived(edge, landing, k):
        @pl.when(band < 15)
        def _():
            halo(edge, landing, k, True).wait_recv()

        @pl.when(band > 0)
        def _():
            halo(edge, landing, k + 1, False).wait_recv()

    halo_arrived(xedge, xhalo, 0)
    xh[:, 0:128], xl[:, 0:128] = halves(xhalo[0])
    xh[:, 640:768], xl[:, 640:768] = halves(xhalo[1])
    slopes = hidden_of((0, 3))
    halo_arrived(yedge, yhalo, 2)
    yh[:, 0:128], yl[:, 0:128] = halves(yhalo[0])
    yh[:, 640:768], yl[:, 640:768] = halves(yhalo[1])
    second_gradient((0, 3), True)

    x_half, x_odd, y_half, y_odd = x // 2, x % 2, y // 2, y % 2

    def first_copies(layer, g):
        copies = []
        for step in (1, 2, 3):
            to = (x + step) % 4
            k = 6 * layer + step - 1
            copies.append(
                remote(
                    g.at[:, :, to % 2, to // 2, to % 2], along_x.at[layer, step - 1],
                    rs_s.at[k], rs_r.at[k], m, y * 4 + to,
                )
            )
            to = (y + step) % 4
            copies.append(
                remote(
                    g.at[:, to // 2, to % 2, :, 1 - to % 2], along_y.at[layer, step - 1],
                    rs_s.at[k + 3], rs_r.at[k + 3], m, to * 4 + x,
                )
            )
        return copies

    def last_copies(layer):
        copies = []
        for half in range(2):
            to = 2 * half + x_odd
            slot = (y - to + 3) % 4
            copies.append((to != y, remote(
                sum_x.at[layer, :, half], landed.at[layer, slot],
                last_s.at[4 * layer + half], last_r.at[3 * layer + slot], m, to * 4 + x,
            )))
            to = 2 * half + 1 - y_odd
            slot = (x - to + 3) % 4
            copies.append((to != x, remote(
                sum_y.at[layer, :, half], landed.at[layer, slot],
                last_s.at[4 * layer + 2 + half], last_r.at[3 * layer + slot], m, y * 4 + to,
            )))
        return copies

    def pass_on(layer, g):
        for c in first_copies(layer, g):
            c.wait_recv()
        sum_x[layer] = g[:, :, x_odd, x_half, x_odd] + (
            along_x[layer, 0] + (along_x[layer, 1] + along_x[layer, 2])
        )
        sum_y[layer] = g[:, y_half, y_odd, :, 1 - y_odd] + (
            along_y[layer, 0] + (along_y[layer, 1] + along_y[layer, 2])
        )
        for going, c in last_copies(layer):
            @pl.when(going)
            def _():
                c.start()

    def take(layer):
        for slot in range(3):
            remote(
                landed.at[layer, slot], landed.at[layer, slot],
                last_s.at[0], last_r.at[3 * layer + slot], m, band,
            ).wait_recv()
        own = jnp.where(x_odd == y_odd, sum_x[layer, :, y_half], sum_y[layer, :, x_half])
        total = own + (landed[layer, 0] + (landed[layer, 1] + landed[layer, 2]))
        for k in range(9):
            sown[layer, k] = total[k // 3, :, 128 * (k % 3) : 128 * (k % 3) + 128]

    for c in first_copies(1, ga):
        c.start()
    first_gradient((0, 3), slopes, True)

    for c in first_copies(0, gb):
        c.start()
    pass_on(1, ga)
    pass_on(0, gb)

    def to_owner(layer):
        return remote(sown.at[layer], held.at[m], c_s.at[layer], c_r.at[0], OWNERS[layer], band)

    def hand_over(layer):
        @pl.when(m != OWNERS[layer])
        def _():
            to_owner(layer).start()

        @pl.when(m == OWNERS[layer])
        def _():
            held[m] = sown[layer]

    take(1)
    hand_over(1)
    take(0)
    hand_over(0)

    def gram_copy(j):
        return remote(gram_b.at[band], gram_b.at[band], d_s.at[j - 1], d_r.at[0], m, (band + j) % 16)

    def block_copy(to):
        return remote(block, block, e1_s.at[to], e1_r.at[0], 2 * to + core, band)

    def finish(layer, alpha):
        totals = [alpha[0:1] * held[0, k] for k in range(9)]
        for q in range(1, 32):
            totals = [v + alpha[q : q + 1] * held[q, k] for k, v in enumerate(totals)]
        for k, v in enumerate(totals):
            t = k if layer == 0 else 3 * (k % 3) + k // 3
            block[pl.ds(t, 8, stride=9), :] = v

    @pl.when(owner)
    def _():
        pltpu.make_async_copy(held.at[pl.ds(0, 31)], held.at[pl.ds(0, 31)], c_r.at[0]).wait()
        flat = held.reshape(2304, 128)
        total = jnp.zeros((96, 96), F32)
        for row in range(0, 72, 4):
            lines = [flat[pl.ds(row + q, 32, stride=72), :] for q in range(4)]
            v = jnp.concatenate(thirds(jnp.concatenate(lines, axis=1)), axis=0)
            total = total + nt(v, v)
        total = total[0:32] + total[32:64] + total[64:96]
        total = total[:, 0:32] + total[:, 32:64] + total[:, 64:96]
        gram_b[band] = jnp.concatenate([total[8 * q : 8 * q + 8] for q in range(4)], axis=1)

        @pl.loop(1, 16)
        def _(j):
            gram_copy(j).start()

        pltpu.make_async_copy(gram_b.at[pl.ds(0, 15)], gram_b.at[pl.ds(0, 15)], d_r.at[0]).wait()
        packed = jnp.sum(gram_b[...], axis=0)
        rows = [packed if q == 0 else pltpu.roll(packed, 128 - 32 * q, 1) for q in range(4)]
        gram = jnp.concatenate(rows, axis=0)
        lane = lax.broadcasted_iota(jnp.int32, gram.shape, 1)
        alpha = adasum_weights(jnp.where(lane < 32, gram, 0.0))
        for layer in range(2):
            @pl.when(core == layer)
            def _():
                finish(layer, alpha)

        for to in ORDER:
            @pl.when(to != depth)
            def _():
                block_copy(to).start()

    @pl.when(jnp.logical_not(owner))
    def _():
        pltpu.make_async_copy(block, block, e1_r.at[0]).wait()

    start = pl.multiple_of(72 * band, 8)
    place = out.at[core, pl.ds(start, 72)]
    own = pltpu.make_async_copy(block, place, loc_sem.at[0])
    own.start()

    @pl.loop(1, 16)
    def _(j):
        remote(block, place, e2_s.at[j - 1], e2_r.at[j - 1], m, (band + j) % 16).start()

    remote(block, place, f_s.at[0], f_r.at[0], sibling, band).start()

    @pl.loop(1, 16)
    def _(j):
        source = (band + 16 - j) % 16
        there = out.at[core, pl.ds(pl.multiple_of(72 * source, 8), 72)]
        remote(block, there, e2_s.at[j - 1], e2_r.at[j - 1], m, band).wait_recv()
        remote(there, there, f_s.at[j], f_r.at[j], sibling, band).start()

    @pl.loop(0, 16)
    def _(j):
        source = (band + 16 - j) % 16
        there = out.at[1 - core, pl.ds(pl.multiple_of(72 * source, 8), 72)]
        copy = remote(block, there, f_s.at[j], f_r.at[j], sibling, band)
        copy.wait_recv()
        copy.wait_send()

    own.wait()

    @pl.loop(1, 16)
    def _(j):
        remote(block, place, e2_s.at[j - 1], e2_r.at[j - 1], m, band).wait_send()

    @pl.when(band > 0)
    def _():
        halo(xedge, xhalo, 0, True).wait_send()
        halo(yedge, yhalo, 2, True).wait_send()

    @pl.when(band < 15)
    def _():
        halo(xedge, xhalo, 1, False).wait_send()
        halo(yedge, yhalo, 3, False).wait_send()

    for layer, g in ((0, gb), (1, ga)):
        for c in first_copies(layer, g):
            c.wait_send()
        for going, c in last_copies(layer):
            @pl.when(going)
            def _():
                c.wait_send()
    for layer in range(2):
        @pl.when(m != OWNERS[layer])
        def _():
            to_owner(layer).wait_send()

    @pl.when(owner)
    def _():
        for to in ORDER:
            @pl.when(to != depth)
            def _():
                block_copy(to).wait_send()

        @pl.loop(1, 16)
        def _(j):
            gram_copy(j).wait_send()


def local(images, cotangent, filters, rates):
    dma = pltpu.SemaphoreType.DMA
    hbm = pl.BlockSpec(memory_space=pltpu.HBM)
    vmem = pltpu.VMEM
    merged = pl.pallas_call(
        kernel,
        out_shape=pltpu.VMEM((2, 1152, 128), F32),
        in_specs=[hbm, hbm, hbm],
        out_specs=pl.BlockSpec(memory_space=pltpu.VMEM),
        scratch_shapes=[
            vmem((512, 128), F32), vmem((512, 128), F32), vmem((2, 1152, 128), F32),
            *[vmem((2, 128, 128), F32)] * 4,
            *[vmem((128, 768), BF16)] * 4,
            *[vmem((384, 384), BF16)] * 4,
            vmem((384, 256), F32),
            *[vmem((384, 256), BF16)] * 2,
            *[vmem((3, 2, 2, 2, 2, 8, 384), F32)] * 2,
            *[vmem((2, 3, 3, 2, 8, 384), F32)] * 2,
            *[vmem((2, 3, 2, 8, 384), F32)] * 2,
            vmem((2, 3, 3, 8, 384), F32),
            vmem((2, 9, 8, 128), F32),
            vmem((32, 9, 8, 128), F32),
            vmem((16, 8, 128), F32),
            vmem((72, 128), F32),
            dma((3,)), dma((4,)), dma((4,)),
            dma((12,)), dma((12,)), dma((8,)), dma((6,)),
            dma((2,)), dma((1,)), dma((15,)), dma((1,)), dma((16,)), dma((1,)),
            dma((15,)), dma((15,)), dma((16,)), dma((16,)), dma((1,)),
        ],
        compiler_params=pltpu.CompilerParams(
            collective_id=0, has_side_effects=True, vmem_limit_bytes=61 * 1024 * 1024
        ),
        name="adasum_step",
    )(images.reshape(512, 128), cotangent.reshape(512, 128), filters)
    return (filters - rates[:, None, None] * merged)[None]


def solution(mesh):
    return jax.shard_map(
        local,
        mesh=mesh,
        in_specs=(P("image", None, "band", None), P("image", None, "band", None), P(), P()),
        out_specs=P("image", None, None, None),
        check_vma=False,
    )
```

```python
import functools

import jax
import jax.numpy as jnp
from jax import lax
from jax.experimental import pallas as pl
from jax.experimental.pallas import tpu as pltpu
from jax.sharding import PartitionSpec as P

MESH = pl.DeviceIdType.MESH
F32 = jnp.float32
BF16 = jnp.bfloat16
HIGH = lax.Precision.HIGHEST


def remote(src, dst, send, recv, image, band):
    return pltpu.make_async_remote_copy(
        src_ref=src,
        dst_ref=dst,
        send_sem=send,
        recv_sem=recv,
        device_id={"image": image, "band": band},
        device_id_type=MESH,
    )


def halves(v):
    hi = v.astype(BF16)
    return hi, (v - hi.astype(F32)).astype(BF16)


def before(v):
    lane = lax.broadcasted_iota(jnp.int32, v.shape, 1)
    return jnp.where(lane == 0, 0.0, pltpu.roll(v, 1, 1))


def after(v):
    lane = lax.broadcasted_iota(jnp.int32, v.shape, 1)
    return jnp.where(lane == 127, 0.0, pltpu.roll(v, 127, 1))


def nn(a, b):
    return lax.dot_general(a, b, (((1,), (0,)), ((), ())), preferred_element_type=F32)


def nt(a, b):
    return lax.dot_general(a, b, (((1,), (1,)), ((), ())), preferred_element_type=F32)


def partner_sum(h, level):
    bit = 1 << level
    if bit >= 8:
        blocks = [h[8 * k : 8 * k + 8] for k in range(4)]
        other = jnp.concatenate([blocks[k ^ (bit // 8)] for k in range(4)], axis=0)
    else:
        blocks = []
        for k in range(4):
            v = h[8 * k : 8 * k + 8]
            r = lax.broadcasted_iota(jnp.int32, v.shape, 0)
            blocks.append(jnp.where((r & bit) == 0, pltpu.roll(v, 8 - bit, 0), pltpu.roll(v, bit, 0)))
        other = jnp.concatenate(blocks, axis=0)
    h = h + other
    lane = lax.broadcasted_iota(jnp.int32, h.shape, 1)
    other = jnp.where((lane & bit) == 0, pltpu.roll(h, 128 - bit, 1), pltpu.roll(h, bit, 1))
    return h + other


def adasum_weights(gram):
    row = lax.broadcasted_iota(jnp.int32, gram.shape, 0)
    lane = lax.broadcasted_iota(jnp.int32, gram.shape, 1)
    alpha = jnp.ones((32, 1), F32)
    for level in range(5):
        own = row == lane
        pair = row == (lane ^ (1 << level))
        sq = jnp.where(own, gram, 0.0)
        inner = jnp.where(pair, gram, 0.0)
        u_col = 1.0 - jnp.sum(inner, axis=1, keepdims=True) / (
            2.0 * (jnp.sum(sq, axis=1, keepdims=True) + 1e-6)
        )
        alpha = alpha * u_col
        if level < 4:
            u_row = 1.0 - jnp.sum(inner, axis=0, keepdims=True) / (
                2.0 * (jnp.sum(sq, axis=0, keepdims=True) + 1e-6)
            )
            gram = partner_sum(gram * u_col * u_row, level)
    return alpha


def thirds(v):
    hi = v.astype(BF16)
    v = v - hi.astype(F32)
    mid = v.astype(BF16)
    return hi, mid, (v - mid.astype(F32)).astype(BF16)


OWNERS = (0, 9)
STEPS = tuple(sorted(
    ((dy, dx) for dy in range(4) for dx in range(4) if dy or dx),
    key=lambda step: -sum(min(d, 4 - d) for d in step),
))
ORDER = (0, 1, 2, 3, 4, 15, 5, 14, 6, 13, 7, 12, 8, 11, 9, 10)


def kernel(
    img_in, cot_in, fil_in, out,
    img, cot, fil, xedge, yedge, xhalo, yhalo, xh, xl, yh, yl, w1h, w1l, w2h, w2l, z, hh, hl,
    ga, gb, along_x, along_y, sum_x, sum_y, landed, sown,
    held, gram_b, block,
    in_sem, halo_s, halo_r, rs_s, rs_r, last_s, last_r,
    c_s, c_r, d_s, d_r, e1_s, e1_r, e2_s, e2_r, f_s, f_r, loc_sem,
):
    m = lax.axis_index("image")
    band = lax.axis_index("band")
    depth, core = m // 2, m % 2
    y, x = band // 4, band % 4
    scale = 1152.0 ** -0.5

    barrier = pltpu.get_barrier_semaphore()

    def tell(sem, image, place):
        pl.semaphore_signal(
            sem, inc=1, device_id={"image": image, "band": place}, device_id_type=MESH
        )

    sibling = m + 1 - 2 * core
    owner = (m == OWNERS[0]) | (m == OWNERS[1])
    beside_owner = (sibling == OWNERS[0]) | (sibling == OWNERS[1])

    @pl.loop(1, 16)
    def _(j):
        tell(barrier, m, (band + j) % 16)

    @pl.when(owner)
    def _():
        @pl.loop(1, 32)
        def _(j):
            tell(barrier, (m + j) % 32, band)

    @pl.when(jnp.logical_not(owner))
    def _():
        tell(barrier, sibling, band)

    loads = [
        pltpu.make_async_copy(src, dst, in_sem.at[k])
        for k, (src, dst) in enumerate(((img_in, img), (cot_in, cot), (fil_in, fil)))
    ]
    for c in loads:
        c.start()

    for c, field, edge in ((loads[0], img, xedge), (loads[1], cot, yedge)):
        c.wait()
        edge[0] = field[pl.ds(0, 128, stride=4), :]
        edge[1] = field[pl.ds(3, 128, stride=4), :]

    def halo(edge, landing, k, up):
        if up:
            return remote(edge.at[0], landing.at[1], halo_s.at[k], halo_r.at[k], m, band - 1)
        return remote(edge.at[1], landing.at[0], halo_s.at[k], halo_r.at[k], m, band + 1)

    @pl.when(owner | beside_owner)
    def _():
        pl.semaphore_wait(barrier, 17)

    @pl.when(jnp.logical_not(owner | beside_owner))
    def _():
        pl.semaphore_wait(barrier, 18)


    @pl.when(band > 0)
    def _():
        halo(xedge, xhalo, 0, True).start()

    @pl.when(band < 15)
    def _():
        halo(xedge, xhalo, 1, False).start()

    @pl.when(band > 0)
    def _():
        halo(yedge, yhalo, 2, True).start()

    @pl.when(band < 15)
    def _():
        halo(yedge, yhalo, 3, False).start()

    for field, vh, vl in ((img, xh, xl), (cot, yh, yl)):
        for r in range(4):
            cols = slice(128 * (r + 1), 128 * (r + 2))
            vh[:, cols], vl[:, cols] = halves(field[pl.ds(r, 128, stride=4), :])

    loads[2].wait()
    for a in range(3):
        for b in range(3):
            rows, cols = slice(128 * b, 128 * b + 128), slice(128 * a, 128 * a + 128)
            w = fil[0, pl.ds(3 * a + b, 128, stride=9), :]
            w1h[rows, cols], w1l[rows, cols] = halves(w.T)
            w2h[rows, cols], w2l[rows, cols] = halves(fil[1, pl.ds(3 * a + b, 128, stride=9), :])

    def columns(ref, pair, offset):
        first, second = (128 * (r + offset) for r in pair)
        return jnp.concatenate([ref[:, first : first + 128], ref[:, second : second + 128]], axis=1)

    def stacked(ref, pair, order):
        return jnp.concatenate([columns(ref, pair, a) for a in order], axis=0)

    def product(wh, wl, hi, lo):
        z[...] = nn(wh[...], hi) + (nn(wh[...], lo) + nn(wl[...], hi))

    def hidden_of(pair):
        product(w1h, w1l, stacked(xh, pair, (0, 1, 2)), stacked(xl, pair, (0, 1, 2)))
        slopes = []
        for q in range(2):
            cols = slice(128 * q, 128 * q + 128)
            pre = scale * (before(z[0:128, cols]) + z[128:256, cols] + after(z[256:384, cols]))
            sig = 1.0 / (1.0 + jnp.exp(-pre))
            hidden = scale * (pre * sig)
            slopes.append((scale * scale) * (sig * (1.0 + pre * (1.0 - sig))))
            for b, v in enumerate((before(hidden), hidden, after(hidden))):
                hh[128 * b : 128 * b + 128, cols], hl[128 * b : 128 * b + 128, cols] = halves(v)
        return slopes

    def second_gradient(pair, add):
        hi, lo = stacked(yh, pair, (2, 1, 0)), stacked(yl, pair, (2, 1, 0))
        for b in range(3):
            rows = slice(128 * b, 128 * b + 128)
            part = nt(hh[rows], hi) + (nt(hh[rows], lo) + nt(hl[rows], hi))
            part = part.reshape(2, 2, 2, 2, 8, 384)
            ga[b] = ga[b] + part if add else part

    def first_gradient(pair, slopes, add):
        product(w2h, w2l, stacked(yh, pair, (2, 1, 0)), stacked(yl, pair, (2, 1, 0)))
        for q in range(2):
            cols = slice(128 * q, 128 * q + 128)
            dpre = (after(z[0:128, cols]) + z[128:256, cols] + before(z[256:384, cols])) * slopes[q]
            for b, v in enumerate((after(dpre), dpre, before(dpre))):
                hh[128 * b : 128 * b + 128, cols], hl[128 * b : 128 * b + 128, cols] = halves(v)
        for a in range(3):
            hi, lo = columns(xh, pair, a), columns(xl, pair, a)
            part = nt(hi, hh[...]) + (nt(hi, hl[...]) + nt(lo, hh[...]))
            part = part.reshape(2, 2, 2, 2, 8, 384)
            gb[a] = gb[a] + part if add else part

    slopes = hidden_of((1, 2))
    second_gradient((1, 2), False)
    first_gradient((1, 2), slopes, False)

    @pl.when(band == 0)
    def _():
        xhalo[0] = jnp.zeros((128, 128), F32)
        yhalo[0] = jnp.zeros((128, 128), F32)

    @pl.when(band == 15)
    def _():
        xhalo[1] = jnp.zeros((128, 128), F32)
        yhalo[1] = jnp.zeros((128, 128), F32)

    def halo_arrived(edge, landing, k):
        @pl.when(band < 15)
        def _():
            halo(edge, landing, k, True).wait_recv()

        @pl.when(band > 0)
        def _():
            halo(edge, landing, k + 1, False).wait_recv()

    halo_arrived(xedge, xhalo, 0)
    xh[:, 0:128], xl[:, 0:128] = halves(xhalo[0])
    xh[:, 640:768], xl[:, 640:768] = halves(xhalo[1])
    slopes = hidden_of((0, 3))
    halo_arrived(yedge, yhalo, 2)
    yh[:, 0:128], yl[:, 0:128] = halves(yhalo[0])
    yh[:, 640:768], yl[:, 640:768] = halves(yhalo[1])
    second_gradient((0, 3), True)

    x_half, x_odd, y_half, y_odd = x // 2, x % 2, y // 2, y % 2

    def first_copies(layer, g):
        copies = []
        for step in (1, 2, 3):
            to = (x + step) % 4
            k = 6 * layer + step - 1
            copies.append(
                remote(
                    g.at[:, :, to % 2, to // 2, to % 2], along_x.at[layer, step - 1],
                    rs_s.at[k], rs_r.at[k], m, y * 4 + to,
                )
            )
            to = (y + step) % 4
            copies.append(
                remote(
                    g.at[:, to // 2, to % 2, :, 1 - to % 2], along_y.at[layer, step - 1],
                    rs_s.at[k + 3], rs_r.at[k + 3], m, to * 4 + x,
                )
            )
        return copies

    def last_copies(layer):
        copies = []
        for half in range(2):
            to = 2 * half + x_odd
            slot = (y - to + 3) % 4
            copies.append((to != y, remote(
                sum_x.at[layer, :, half], landed.at[layer, slot],
                last_s.at[4 * layer + half], last_r.at[3 * layer + slot], m, to * 4 + x,
            )))
            to = 2 * half + 1 - y_odd
            slot = (x - to + 3) % 4
            copies.append((to != x, remote(
                sum_y.at[layer, :, half], landed.at[layer, slot],
                last_s.at[4 * layer + 2 + half], last_r.at[3 * layer + slot], m, y * 4 + to,
            )))
        return copies

    def pass_on(layer, g):
        arriving, leaving = first_copies(layer, g), last_copies(layer)
        for route in range(2):
            for c in arriving[route::2]:
                c.wait_recv()
            if route == 0:
                sum_x[layer] = g[:, :, x_odd, x_half, x_odd] + (
                    along_x[layer, 0] + (along_x[layer, 1] + along_x[layer, 2])
                )
            else:
                sum_y[layer] = g[:, y_half, y_odd, :, 1 - y_odd] + (
                    along_y[layer, 0] + (along_y[layer, 1] + along_y[layer, 2])
                )
            for going, c in leaving[route::2]:
                @pl.when(going)
                def _():
                    c.start()

    def take(layer):
        for slot in range(3):
            remote(
                landed.at[layer, slot], landed.at[layer, slot],
                last_s.at[0], last_r.at[3 * layer + slot], m, band,
            ).wait_recv()
        own = jnp.where(x_odd == y_odd, sum_x[layer, :, y_half], sum_y[layer, :, x_half])
        total = own + (landed[layer, 0] + (landed[layer, 1] + landed[layer, 2]))
        for k in range(9):
            sown[layer, k] = total[k // 3, :, 128 * (k % 3) : 128 * (k % 3) + 128]

    for c in first_copies(1, ga):
        c.start()
    first_gradient((0, 3), slopes, True)

    for c in first_copies(0, gb):
        c.start()
    pass_on(1, ga)
    pass_on(0, gb)

    def to_owner(layer):
        return remote(sown.at[layer], held.at[m], c_s.at[layer], c_r.at[0], OWNERS[layer], band)

    def hand_over(layer):
        @pl.when(m != OWNERS[layer])
        def _():
            to_owner(layer).start()

        @pl.when(m == OWNERS[layer])
        def _():
            held[m] = sown[layer]

    take(1)
    hand_over(1)
    take(0)
    hand_over(0)

    @pl.when(band > 0)
    def _():
        halo(xedge, xhalo, 0, True).wait_send()
        halo(yedge, yhalo, 2, True).wait_send()

    @pl.when(band < 15)
    def _():
        halo(xedge, xhalo, 1, False).wait_send()
        halo(yedge, yhalo, 3, False).wait_send()

    for layer, g in ((0, gb), (1, ga)):
        for c in first_copies(layer, g):
            c.wait_send()
        for going, c in last_copies(layer):
            @pl.when(going)
            def _():
                c.wait_send()
    for layer in range(2):
        @pl.when(m != OWNERS[layer])
        def _():
            to_owner(layer).wait_send()

    def peer(dy, dx):
        return ((y + dy + 4) % 4) * 4 + (x + dx + 4) % 4

    def gram_copy(k):
        return remote(gram_b.at[band], gram_b.at[band], d_s.at[k], d_r.at[0], m, peer(*STEPS[k]))

    def block_copy(to):
        return remote(block, block, e1_s.at[to], e1_r.at[0], 2 * to + core, band)

    def finish(layer, alpha):
        totals = [alpha[0:1] * held[0, k] for k in range(9)]
        for q in range(1, 32):
            totals = [v + alpha[q : q + 1] * held[q, k] for k, v in enumerate(totals)]
        for k, v in enumerate(totals):
            t = k if layer == 0 else 3 * (k % 3) + k // 3
            block[pl.ds(t, 8, stride=9), :] = v

    @pl.when(owner)
    def _():
        pltpu.make_async_copy(held.at[pl.ds(0, 31)], held.at[pl.ds(0, 31)], c_r.at[0]).wait()
        flat = held.reshape(2304, 128)
        total = jnp.zeros((96, 96), F32)
        for row in range(0, 72, 4):
            lines = [flat[pl.ds(row + q, 32, stride=72), :] for q in range(4)]
            v = jnp.concatenate(thirds(jnp.concatenate(lines, axis=1)), axis=0)
            total = total + nt(v, v)
        total = total[0:32] + total[32:64] + total[64:96]
        total = total[:, 0:32] + total[:, 32:64] + total[:, 64:96]
        gram_b[band] = jnp.concatenate([total[8 * q : 8 * q + 8] for q in range(4)], axis=1)

        for k in range(15):
            gram_copy(k).start()

        pltpu.make_async_copy(gram_b.at[pl.ds(0, 15)], gram_b.at[pl.ds(0, 15)], d_r.at[0]).wait()
        packed = jnp.sum(gram_b[...], axis=0)
        rows = [packed if q == 0 else pltpu.roll(packed, 128 - 32 * q, 1) for q in range(4)]
        gram = jnp.concatenate(rows, axis=0)
        lane = lax.broadcasted_iota(jnp.int32, gram.shape, 1)
        alpha = adasum_weights(jnp.where(lane < 32, gram, 0.0))
        for layer in range(2):
            @pl.when(core == layer)
            def _():
                finish(layer, alpha)

        for to in ORDER:
            @pl.when(to != depth)
            def _():
                block_copy(to).start()

    @pl.when(jnp.logical_not(owner))
    def _():
        pltpu.make_async_copy(block, block, e1_r.at[0]).wait()

    start = pl.multiple_of(72 * band, 8)
    place = out.at[core, pl.ds(start, 72)]
    own = pltpu.make_async_copy(block, place, loc_sem.at[0])
    own.start()

    def rows_of(layer, source):
        return out.at[layer, pl.ds(pl.multiple_of(72 * source, 8), 72)]

    def to_band(k, dy, dx):
        return remote(block, place, e2_s.at[k], e2_r.at[k], m, peer(dy, dx))

    for k, (dy, dx) in enumerate(STEPS):
        to_band(k, dy, dx).start()
    remote(block, place, f_s.at[15], f_r.at[15], sibling, band).start()

    for k, (dy, dx) in enumerate(STEPS):
        there = rows_of(core, peer(-dy, -dx))
        remote(block, there, e2_s.at[k], e2_r.at[k], m, band).wait_recv()
        remote(there, there, f_s.at[k], f_r.at[k], sibling, band).start()

    for k, (dy, dx) in enumerate((*STEPS, (0, 0))):
        there = rows_of(1 - core, peer(-dy, -dx))
        copy = remote(block, there, f_s.at[k], f_r.at[k], sibling, band)
        copy.wait_recv()
        copy.wait_send()

    own.wait()
    for k, (dy, dx) in enumerate(STEPS):
        to_band(k, dy, dx).wait_send()

    @pl.when(owner)
    def _():
        for to in ORDER:
            @pl.when(to != depth)
            def _():
                block_copy(to).wait_send()

        for k in range(15):
            gram_copy(k).wait_send()


def local(images, cotangent, filters, rates):
    dma = pltpu.SemaphoreType.DMA
    hbm = pl.BlockSpec(memory_space=pltpu.HBM)
    vmem = pltpu.VMEM
    merged = pl.pallas_call(
        kernel,
        out_shape=pltpu.VMEM((2, 1152, 128), F32),
        in_specs=[hbm, hbm, hbm],
        out_specs=pl.BlockSpec(memory_space=pltpu.VMEM),
        scratch_shapes=[
            vmem((512, 128), F32), vmem((512, 128), F32), vmem((2, 1152, 128), F32),
            *[vmem((2, 128, 128), F32)] * 4,
            *[vmem((128, 768), BF16)] * 4,
            *[vmem((384, 384), BF16)] * 4,
            vmem((384, 256), F32),
            *[vmem((384, 256), BF16)] * 2,
            *[vmem((3, 2, 2, 2, 2, 8, 384), F32)] * 2,
            *[vmem((2, 3, 3, 2, 8, 384), F32)] * 2,
            *[vmem((2, 3, 2, 8, 384), F32)] * 2,
            vmem((2, 3, 3, 8, 384), F32),
            vmem((2, 9, 8, 128), F32),
            vmem((32, 9, 8, 128), F32),
            vmem((16, 8, 128), F32),
            vmem((72, 128), F32),
            dma((3,)), dma((4,)), dma((4,)),
            dma((12,)), dma((12,)), dma((8,)), dma((6,)),
            dma((2,)), dma((1,)), dma((15,)), dma((1,)), dma((16,)), dma((1,)),
            dma((15,)), dma((15,)), dma((16,)), dma((16,)), dma((1,)),
        ],
        compiler_params=pltpu.CompilerParams(
            collective_id=0, has_side_effects=True, vmem_limit_bytes=61 * 1024 * 1024
        ),
        name="adasum_step",
    )(images.reshape(512, 128), cotangent.reshape(512, 128), filters)
    return (filters - rates[:, None, None] * merged)[None]


def solution(mesh):
    return jax.shard_map(
        local,
        mesh=mesh,
        in_specs=(P("image", None, "band", None), P("image", None, "band", None), P(), P()),
        out_specs=P("image", None, None, None),
        check_vma=False,
    )
```

```python
import functools

import jax
import jax.numpy as jnp
from jax import lax
from jax.experimental import pallas as pl
from jax.experimental.pallas import tpu as pltpu
from jax.sharding import PartitionSpec as P

MESH = pl.DeviceIdType.MESH
F32 = jnp.float32
BF16 = jnp.bfloat16
HIGH = lax.Precision.HIGHEST


def remote(src, dst, send, recv, image, band):
    return pltpu.make_async_remote_copy(
        src_ref=src,
        dst_ref=dst,
        send_sem=send,
        recv_sem=recv,
        device_id={"image": image, "band": band},
        device_id_type=MESH,
    )


def halves(v):
    hi = v.astype(BF16)
    return hi, (v - hi.astype(F32)).astype(BF16)


def before(v):
    lane = lax.broadcasted_iota(jnp.int32, v.shape, 1)
    return jnp.where(lane == 0, 0.0, pltpu.roll(v, 1, 1))


def after(v):
    lane = lax.broadcasted_iota(jnp.int32, v.shape, 1)
    return jnp.where(lane == 127, 0.0, pltpu.roll(v, 127, 1))


def nn(a, b):
    return lax.dot_general(a, b, (((1,), (0,)), ((), ())), preferred_element_type=F32)


def nt(a, b):
    return lax.dot_general(a, b, (((1,), (1,)), ((), ())), preferred_element_type=F32)


def partner_sum(h, level):
    bit = 1 << level
    if bit >= 8:
        blocks = [h[8 * k : 8 * k + 8] for k in range(4)]
        other = jnp.concatenate([blocks[k ^ (bit // 8)] for k in range(4)], axis=0)
    else:
        blocks = []
        for k in range(4):
            v = h[8 * k : 8 * k + 8]
            r = lax.broadcasted_iota(jnp.int32, v.shape, 0)
            blocks.append(jnp.where((r & bit) == 0, pltpu.roll(v, 8 - bit, 0), pltpu.roll(v, bit, 0)))
        other = jnp.concatenate(blocks, axis=0)
    h = h + other
    lane = lax.broadcasted_iota(jnp.int32, h.shape, 1)
    other = jnp.where((lane & bit) == 0, pltpu.roll(h, 128 - bit, 1), pltpu.roll(h, bit, 1))
    return h + other


def adasum_weights(gram):
    row = lax.broadcasted_iota(jnp.int32, gram.shape, 0)
    lane = lax.broadcasted_iota(jnp.int32, gram.shape, 1)
    alpha = jnp.ones((32, 1), F32)
    for level in range(5):
        own = row == lane
        pair = row == (lane ^ (1 << level))
        sq = jnp.where(own, gram, 0.0)
        inner = jnp.where(pair, gram, 0.0)
        u_col = 1.0 - jnp.sum(inner, axis=1, keepdims=True) / (
            2.0 * (jnp.sum(sq, axis=1, keepdims=True) + 1e-6)
        )
        alpha = alpha * u_col
        if level < 4:
            u_row = 1.0 - jnp.sum(inner, axis=0, keepdims=True) / (
                2.0 * (jnp.sum(sq, axis=0, keepdims=True) + 1e-6)
            )
            gram = partner_sum(gram * u_col * u_row, level)
    return alpha


def thirds(v):
    hi = v.astype(BF16)
    v = v - hi.astype(F32)
    mid = v.astype(BF16)
    return hi, mid, (v - mid.astype(F32)).astype(BF16)


OWNERS = (0, 9)
STEPS = tuple(sorted(
    ((dy, dx) for dy in range(4) for dx in range(4) if dy or dx),
    key=lambda step: -sum(min(d, 4 - d) for d in step),
))
ORDER = (0, 1, 2, 3, 4, 15, 5, 14, 6, 13, 7, 12, 8, 11, 9, 10)


def kernel(
    img_in, cot_in, fil_in, out,
    img, cot, fil, xedge, yedge, xhalo, yhalo, xh, xl, yh, yl, w1h, w1l, w2h, w2l, z, hh, hl,
    ga, gb, along_x, along_y, sum_x, sum_y, landed, sown,
    held, gram_b, block,
    in_sem, halo_s, halo_r, rs_s, rs_r, last_s, last_r,
    c_s, c_r, d_s, d_r, e1_s, e1_r, e2_s, e2_r, f_s, f_r, loc_sem,
):
    m = lax.axis_index("image")
    band = lax.axis_index("band")
    depth, core = m // 2, m % 2
    y, x = band // 4, band % 4
    scale = 1152.0 ** -0.5

    barrier = pltpu.get_barrier_semaphore()

    def tell(sem, image, place):
        pl.semaphore_signal(
            sem, inc=1, device_id={"image": image, "band": place}, device_id_type=MESH
        )

    sibling = m + 1 - 2 * core
    owner = (m == OWNERS[0]) | (m == OWNERS[1])
    beside_owner = (sibling == OWNERS[0]) | (sibling == OWNERS[1])

    @pl.loop(1, 16)
    def _(j):
        tell(barrier, m, (band + j) % 16)

    @pl.when(owner)
    def _():
        @pl.loop(1, 32)
        def _(j):
            tell(barrier, (m + j) % 32, band)

    @pl.when(jnp.logical_not(owner))
    def _():
        tell(barrier, sibling, band)

    loads = [
        pltpu.make_async_copy(src, dst, in_sem.at[k])
        for k, (src, dst) in enumerate(((img_in, img), (cot_in, cot), (fil_in, fil)))
    ]
    for c in loads:
        c.start()

    for c, field, edge in ((loads[0], img, xedge), (loads[1], cot, yedge)):
        c.wait()
        edge[0] = field[pl.ds(0, 128, stride=4), :]
        edge[1] = field[pl.ds(3, 128, stride=4), :]

    def halo(edge, landing, k, up):
        if up:
            return remote(edge.at[0], landing.at[1], halo_s.at[k], halo_r.at[k], m, band - 1)
        return remote(edge.at[1], landing.at[0], halo_s.at[k], halo_r.at[k], m, band + 1)

    @pl.when(owner | beside_owner)
    def _():
        pl.semaphore_wait(barrier, 17)

    @pl.when(jnp.logical_not(owner | beside_owner))
    def _():
        pl.semaphore_wait(barrier, 18)


    @pl.when(band > 0)
    def _():
        halo(xedge, xhalo, 0, True).start()

    @pl.when(band < 15)
    def _():
        halo(xedge, xhalo, 1, False).start()

    @pl.when(band > 0)
    def _():
        halo(yedge, yhalo, 2, True).start()

    @pl.when(band < 15)
    def _():
        halo(yedge, yhalo, 3, False).start()

    for field, vh, vl in ((img, xh, xl), (cot, yh, yl)):
        for r in range(4):
            cols = slice(128 * (r + 1), 128 * (r + 2))
            vh[:, cols], vl[:, cols] = halves(field[pl.ds(r, 128, stride=4), :])

    loads[2].wait()
    for a in range(3):
        for b in range(3):
            rows, cols = slice(128 * b, 128 * b + 128), slice(128 * a, 128 * a + 128)
            w = fil[0, pl.ds(3 * a + b, 128, stride=9), :]
            w1h[rows, cols], w1l[rows, cols] = halves(w.T)
            w2h[rows, cols], w2l[rows, cols] = halves(fil[1, pl.ds(3 * a + b, 128, stride=9), :])

    def columns(ref, pair, offset):
        first, second = (128 * (r + offset) for r in pair)
        return jnp.concatenate([ref[:, first : first + 128], ref[:, second : second + 128]], axis=1)

    def stacked(ref, pair, order):
        return jnp.concatenate([columns(ref, pair, a) for a in order], axis=0)

    def product(wh, wl, hi, lo):
        z[...] = nn(wh[...], hi) + (nn(wh[...], lo) + nn(wl[...], hi))

    def hidden_of(pair):
        product(w1h, w1l, stacked(xh, pair, (0, 1, 2)), stacked(xl, pair, (0, 1, 2)))
        slopes = []
        for q in range(2):
            cols = slice(128 * q, 128 * q + 128)
            pre = scale * (before(z[0:128, cols]) + z[128:256, cols] + after(z[256:384, cols]))
            sig = 1.0 / (1.0 + jnp.exp(-pre))
            hidden = scale * (pre * sig)
            slopes.append((scale * scale) * (sig * (1.0 + pre * (1.0 - sig))))
            for b, v in enumerate((before(hidden), hidden, after(hidden))):
                hh[128 * b : 128 * b + 128, cols], hl[128 * b : 128 * b + 128, cols] = halves(v)
        return slopes

    def second_gradient(pair, add):
        hi, lo = stacked(yh, pair, (2, 1, 0)), stacked(yl, pair, (2, 1, 0))
        for b in range(3):
            rows = slice(128 * b, 128 * b + 128)
            part = nt(hh[rows], hi) + (nt(hh[rows], lo) + nt(hl[rows], hi))
            part = part.reshape(2, 2, 2, 2, 8, 384)
            ga[b] = ga[b] + part if add else part

    def first_gradient(pair, slopes, add):
        product(w2h, w2l, stacked(yh, pair, (2, 1, 0)), stacked(yl, pair, (2, 1, 0)))
        for q in range(2):
            cols = slice(128 * q, 128 * q + 128)
            dpre = (after(z[0:128, cols]) + z[128:256, cols] + before(z[256:384, cols])) * slopes[q]
            for b, v in enumerate((after(dpre), dpre, before(dpre))):
                hh[128 * b : 128 * b + 128, cols], hl[128 * b : 128 * b + 128, cols] = halves(v)
        for a in range(3):
            hi, lo = columns(xh, pair, a), columns(xl, pair, a)
            part = nt(hi, hh[...]) + (nt(hi, hl[...]) + nt(lo, hh[...]))
            part = part.reshape(2, 2, 2, 2, 8, 384)
            gb[a] = gb[a] + part if add else part

    slopes = hidden_of((1, 2))
    second_gradient((1, 2), False)
    first_gradient((1, 2), slopes, False)

    @pl.when(band == 0)
    def _():
        xhalo[0] = jnp.zeros((128, 128), F32)
        yhalo[0] = jnp.zeros((128, 128), F32)

    @pl.when(band == 15)
    def _():
        xhalo[1] = jnp.zeros((128, 128), F32)
        yhalo[1] = jnp.zeros((128, 128), F32)

    def halo_arrived(edge, landing, k):
        @pl.when(band < 15)
        def _():
            halo(edge, landing, k, True).wait_recv()

        @pl.when(band > 0)
        def _():
            halo(edge, landing, k + 1, False).wait_recv()

    halo_arrived(xedge, xhalo, 0)
    xh[:, 0:128], xl[:, 0:128] = halves(xhalo[0])
    xh[:, 640:768], xl[:, 640:768] = halves(xhalo[1])
    slopes = hidden_of((0, 3))
    halo_arrived(yedge, yhalo, 2)
    yh[:, 0:128], yl[:, 0:128] = halves(yhalo[0])
    yh[:, 640:768], yl[:, 640:768] = halves(yhalo[1])
    second_gradient((0, 3), True)

    x_half, x_odd, y_half, y_odd = x // 2, x % 2, y // 2, y % 2

    def first_copies(layer, g):
        copies = []
        for step in (2, 1, 3):
            to = (x + step) % 4
            k = 6 * layer + step - 1
            copies.append(
                remote(
                    g.at[:, :, to % 2, to // 2, to % 2], along_x.at[layer, step - 1],
                    rs_s.at[k], rs_r.at[k], m, y * 4 + to,
                )
            )
            to = (y + step) % 4
            copies.append(
                remote(
                    g.at[:, to // 2, to % 2, :, 1 - to % 2], along_y.at[layer, step - 1],
                    rs_s.at[k + 3], rs_r.at[k + 3], m, to * 4 + x,
                )
            )
        return copies

    def last_copies(layer):
        copies = []
        for half in range(2):
            to = 2 * half + x_odd
            slot = (y - to + 3) % 4
            copies.append((to != y, remote(
                sum_x.at[layer, :, half], landed.at[layer, slot],
                last_s.at[4 * layer + half], last_r.at[3 * layer + slot], m, to * 4 + x,
            )))
            to = 2 * half + 1 - y_odd
            slot = (x - to + 3) % 4
            copies.append((to != x, remote(
                sum_y.at[layer, :, half], landed.at[layer, slot],
                last_s.at[4 * layer + 2 + half], last_r.at[3 * layer + slot], m, y * 4 + to,
            )))
        return copies

    def pass_on(layer, g):
        arriving, leaving = first_copies(layer, g), last_copies(layer)
        for route in range(2):
            for c in arriving[route::2]:
                c.wait_recv()
            if route == 0:
                sum_x[layer] = g[:, :, x_odd, x_half, x_odd] + (
                    along_x[layer, 0] + (along_x[layer, 1] + along_x[layer, 2])
                )
            else:
                sum_y[layer] = g[:, y_half, y_odd, :, 1 - y_odd] + (
                    along_y[layer, 0] + (along_y[layer, 1] + along_y[layer, 2])
                )
            for going, c in leaving[route::2]:
                @pl.when(going)
                def _():
                    c.start()

    def take(layer):
        for slot in range(3):
            remote(
                landed.at[layer, slot], landed.at[layer, slot],
                last_s.at[0], last_r.at[3 * layer + slot], m, band,
            ).wait_recv()
        own = jnp.where(x_odd == y_odd, sum_x[layer, :, y_half], sum_y[layer, :, x_half])
        total = own + (landed[layer, 0] + (landed[layer, 1] + landed[layer, 2]))
        for k in range(9):
            sown[layer, k] = total[k // 3, :, 128 * (k % 3) : 128 * (k % 3) + 128]

    for c in first_copies(1, ga):
        c.start()
    first_gradient((0, 3), slopes, True)

    for c in first_copies(0, gb):
        c.start()
    pass_on(1, ga)
    pass_on(0, gb)

    def to_owner(layer):
        return remote(sown.at[layer], held.at[m], c_s.at[layer], c_r.at[0], OWNERS[layer], band)

    def hand_over(layer):
        @pl.when(m != OWNERS[layer])
        def _():
            to_owner(layer).start()

        @pl.when(m == OWNERS[layer])
        def _():
            held[m] = sown[layer]

    take(1)
    hand_over(1)
    take(0)
    hand_over(0)

    @pl.when(band > 0)
    def _():
        halo(xedge, xhalo, 0, True).wait_send()
        halo(yedge, yhalo, 2, True).wait_send()

    @pl.when(band < 15)
    def _():
        halo(xedge, xhalo, 1, False).wait_send()
        halo(yedge, yhalo, 3, False).wait_send()

    for layer, g in ((0, gb), (1, ga)):
        for c in first_copies(layer, g):
            c.wait_send()
        for going, c in last_copies(layer):
            @pl.when(going)
            def _():
                c.wait_send()
    for layer in range(2):
        @pl.when(m != OWNERS[layer])
        def _():
            to_owner(layer).wait_send()

    def peer(dy, dx):
        return ((y + dy + 4) % 4) * 4 + (x + dx + 4) % 4

    def gram_copy(k):
        return remote(gram_b.at[band], gram_b.at[band], d_s.at[k], d_r.at[0], m, peer(*STEPS[k]))

    def block_copy(to):
        return remote(block, block, e1_s.at[to], e1_r.at[0], 2 * to + core, band)

    def finish(layer, alpha):
        totals = [alpha[0:1] * held[0, k] for k in range(9)]
        for q in range(1, 32):
            totals = [v + alpha[q : q + 1] * held[q, k] for k, v in enumerate(totals)]
        for k, v in enumerate(totals):
            t = k if layer == 0 else 3 * (k % 3) + k // 3
            block[pl.ds(t, 8, stride=9), :] = v

    @pl.when(owner)
    def _():
        pltpu.make_async_copy(held.at[pl.ds(0, 31)], held.at[pl.ds(0, 31)], c_r.at[0]).wait()
        flat = held.reshape(2304, 128)
        total = jnp.zeros((96, 96), F32)
        for row in range(0, 72, 4):
            lines = [flat[pl.ds(row + q, 32, stride=72), :] for q in range(4)]
            v = jnp.concatenate(thirds(jnp.concatenate(lines, axis=1)), axis=0)
            total = total + nt(v, v)
        total = total[0:32] + total[32:64] + total[64:96]
        total = total[:, 0:32] + total[:, 32:64] + total[:, 64:96]
        gram_b[band] = jnp.concatenate([total[8 * q : 8 * q + 8] for q in range(4)], axis=1)

        for k in range(15):
            gram_copy(k).start()

        pltpu.make_async_copy(gram_b.at[pl.ds(0, 15)], gram_b.at[pl.ds(0, 15)], d_r.at[0]).wait()
        packed = jnp.sum(gram_b[...], axis=0)
        rows = [packed if q == 0 else pltpu.roll(packed, 128 - 32 * q, 1) for q in range(4)]
        gram = jnp.concatenate(rows, axis=0)
        lane = lax.broadcasted_iota(jnp.int32, gram.shape, 1)
        alpha = adasum_weights(jnp.where(lane < 32, gram, 0.0))
        for layer in range(2):
            @pl.when(core == layer)
            def _():
                finish(layer, alpha)

        for to in ORDER:
            @pl.when(to != depth)
            def _():
                block_copy(to).start()

    @pl.when(jnp.logical_not(owner))
    def _():
        pltpu.make_async_copy(block, block, e1_r.at[0]).wait()

    start = pl.multiple_of(72 * band, 8)
    place = out.at[core, pl.ds(start, 72)]
    own = pltpu.make_async_copy(block, place, loc_sem.at[0])
    own.start()

    def rows_of(layer, source):
        return out.at[layer, pl.ds(pl.multiple_of(72 * source, 8), 72)]

    def to_band(k, dy, dx):
        return remote(block, place, e2_s.at[k], e2_r.at[k], m, peer(dy, dx))

    for k, (dy, dx) in enumerate(STEPS):
        to_band(k, dy, dx).start()
    remote(block, place, f_s.at[15], f_r.at[15], sibling, band).start()

    for k, (dy, dx) in enumerate(STEPS):
        there = rows_of(core, peer(-dy, -dx))
        remote(block, there, e2_s.at[k], e2_r.at[k], m, band).wait_recv()
        remote(there, there, f_s.at[k], f_r.at[k], sibling, band).start()

    for k, (dy, dx) in enumerate((*STEPS, (0, 0))):
        there = rows_of(1 - core, peer(-dy, -dx))
        copy = remote(block, there, f_s.at[k], f_r.at[k], sibling, band)
        copy.wait_recv()
        copy.wait_send()

    own.wait()
    for k, (dy, dx) in enumerate(STEPS):
        to_band(k, dy, dx).wait_send()

    @pl.when(owner)
    def _():
        for to in ORDER:
            @pl.when(to != depth)
            def _():
                block_copy(to).wait_send()

        for k in range(15):
            gram_copy(k).wait_send()


def local(images, cotangent, filters, rates):
    dma = pltpu.SemaphoreType.DMA
    hbm = pl.BlockSpec(memory_space=pltpu.HBM)
    vmem = pltpu.VMEM
    merged = pl.pallas_call(
        kernel,
        out_shape=pltpu.VMEM((2, 1152, 128), F32),
        in_specs=[hbm, hbm, hbm],
        out_specs=pl.BlockSpec(memory_space=pltpu.VMEM),
        scratch_shapes=[
            vmem((512, 128), F32), vmem((512, 128), F32), vmem((2, 1152, 128), F32),
            *[vmem((2, 128, 128), F32)] * 4,
            *[vmem((128, 768), BF16)] * 4,
            *[vmem((384, 384), BF16)] * 4,
            vmem((384, 256), F32),
            *[vmem((384, 256), BF16)] * 2,
            *[vmem((3, 2, 2, 2, 2, 8, 384), F32)] * 2,
            *[vmem((2, 3, 3, 2, 8, 384), F32)] * 2,
            *[vmem((2, 3, 2, 8, 384), F32)] * 2,
            vmem((2, 3, 3, 8, 384), F32),
            vmem((2, 9, 8, 128), F32),
            vmem((32, 9, 8, 128), F32),
            vmem((16, 8, 128), F32),
            vmem((72, 128), F32),
            dma((3,)), dma((4,)), dma((4,)),
            dma((12,)), dma((12,)), dma((8,)), dma((6,)),
            dma((2,)), dma((1,)), dma((15,)), dma((1,)), dma((16,)), dma((1,)),
            dma((15,)), dma((15,)), dma((16,)), dma((16,)), dma((1,)),
        ],
        compiler_params=pltpu.CompilerParams(
            collective_id=0, has_side_effects=True, vmem_limit_bytes=61 * 1024 * 1024
        ),
        name="adasum_step",
    )(images.reshape(512, 128), cotangent.reshape(512, 128), filters)
    return (filters - rates[:, None, None] * merged)[None]


def solution(mesh):
    return jax.shard_map(
        local,
        mesh=mesh,
        in_specs=(P("image", None, "band", None), P("image", None, "band", None), P(), P()),
        out_specs=P("image", None, None, None),
        check_vma=False,
    )
```
